256 devices in a mesh: seq: 32 (over y_hi, z, core), chan: 8 (over y_lo, x).
Axes of the slice: x: 4, y: 4 (y_hi: 2, y_lo: 2; y = y_hi * 2 + y_lo), z: 8, core: 2. Of those that a mesh axis runs over, the one named last changes fastest.
Arguments:
- streams: bfloat16 [3, 256, 524288], P(None, 'chan', 'seq'), may hold values from -6 to 6
- conv_weights: float32 [3, 256, 3], P(None, 'chan'), may hold values from -3.5 to 3.5
- skip: float32 [256], P('chan'), may hold values from 0.5 to 1.5
- filter_spec: bfloat16 [8, 32, 2, 1048576], P('chan', 'seq'), may hold values from -6 to 6
- residual: bfloat16 [256, 524288], P('chan', 'seq'), may hold values from -27 to 27
- gain: float32 [256], P('chan'), may hold values from 0.5 to 1.5
Outputs:
- hidden_out: bfloat16 [256, 524288], P('chan', 'seq')
- normed: bfloat16 [256, 524288], P('chan', 'seq')
The draws below stay inside these ranges and needn't reach their ends.
All inputs are finite; a program needn't handle non-finite values.
Results may differ from the reference program's by a relative error of at most 0.015.
Values may be sent and summed in bfloat16 or wider, within the bound.
A program may use at most 128 MiB of HBM per device.

```python
import math
import jax
import jax.numpy as jnp
from jax import lax

SEQLEN = 524288
FFT_LEN = 1048576
CONV_TAPS = 3
CH_DEV = 32
GROUPS = 8
CHANNELS = 256


def draw_residual(key, part):
    key = jax.random.fold_in(key, 7)
    key_base, key_chan = jax.random.split(key, 2)
    base = jnp.clip(jax.random.normal(key_base, (CHANNELS, SEQLEN), jnp.float32), -4.0, 4.0)
    ramp = 0.5 * 3.0 ** (jnp.arange(CHANNELS, dtype=jnp.float32) / (CHANNELS - 1))
    jitter = jnp.exp(jax.random.uniform(key_chan, (CHANNELS,), jnp.float32, 0.0, math.log(1.5)))
    values = base * (ramp * jitter)[:, None]
    return values.astype(jnp.bfloat16)


def block_levels(key, dims, shards, least, high):
    level = 1.0
    for dim, parts in shards:
        steps = jax.random.uniform(jax.random.fold_in(jax.random.fold_in(key, 6), dim), (parts,), jnp.float32, least / len(shards), high / len(shards))
        level = level * jnp.repeat(jnp.exp(steps), dims[dim] // parts).reshape((-1,) + (1,) * (len(dims) - 1 - dim))
    return level


def bell_draw(key, dims, spread, bound, shards=(), held_as=jnp.bfloat16):
    drawn = spread * jax.random.normal(key, dims, jnp.float32)
    if shards:
        drawn = drawn * block_levels(key, dims, shards, -0.22, 0.18)
    return jnp.clip(drawn, -bound, bound).astype(held_as)


def setup_inputs(seed: int = 0) -> dict:
    seeds = jax.random.split(jax.random.key(seed), 7)
    return {
        "streams": bell_draw(seeds[0], (3, CHANNELS, SEQLEN), 1.0, 6.0, ((1, 8), (2, 32))),
        "conv_weights": bell_draw(seeds[1], (3, CHANNELS, CONV_TAPS), CONV_TAPS ** -0.5, 3.5, ((1, 8),), jnp.float32),
        "skip": jnp.clip(0.5 + 1.0 * jax.random.uniform(seeds[2], (CHANNELS,), jnp.float32) ** block_levels(seeds[2], (CHANNELS,), ((0, 8),), -0.2, 0.2), 0.5, 1.5),
        "filter_spec": bell_draw(seeds[3], (GROUPS, CH_DEV, 2, FFT_LEN), 1.0, 6.0, ((0, 8), (1, 32))),
        "residual": draw_residual(jax.random.fold_in(seeds[6], 71), 0),
        "gain": jnp.clip(1.0 + 0.1 * jax.random.normal(seeds[5], (CHANNELS,), jnp.float32), 0.5, 1.5),
    }


def causal_conv(values, weights):
    kernel_len = weights.shape[1]
    span_len = values.shape[1]
    padded = jnp.pad(values, ((0, 0), (kernel_len - 1, 0)))
    running = jnp.zeros(values.shape, jnp.float32)
    for offset in range(kernel_len):
        begin_at = kernel_len - 1 - offset
        running = running + weights[:, offset:offset + 1] * padded[:, begin_at:begin_at + span_len]
    return running

def one_channel(packed):
    signal, spectrum, weight = packed
    signal_f = signal.astype(jnp.float32)
    padded = jnp.concatenate([signal_f, jnp.zeros((FFT_LEN - SEQLEN,), jnp.float32)])
    forward = jnp.fft.fft(padded)
    product = forward * (spectrum[0] + 1j * spectrum[1])
    inverse = jnp.real(jnp.fft.ifft(product))[:SEQLEN]
    return inverse + weight * signal_f

def reference(streams, conv_weights, skip, filter_spec, residual, gain):
    filtered = [causal_conv(streams[stream_idx].astype(jnp.float32), conv_weights[stream_idx]) for stream_idx in range(3)]
    gate_out = filtered[0].astype(jnp.bfloat16)
    gated_input = (filtered[1] * filtered[2]).astype(jnp.bfloat16)
    spectra = filter_spec.reshape(CHANNELS, 2, FFT_LEN).astype(jnp.float32)
    long_out = lax.map(one_channel, (gated_input, spectra, skip)).astype(jnp.bfloat16)
    hidden_out = (residual.astype(jnp.float32) + gate_out.astype(jnp.float32) * long_out.astype(jnp.float32)).astype(jnp.bfloat16)
    hidden_f = hidden_out.astype(jnp.float32)
    mean_sq = lax.optimization_barrier(jnp.mean(hidden_f * hidden_f, axis=0))
    normed = (hidden_f * gain[:, None] * lax.rsqrt(mean_sq + 1e-06)[None, :]).astype(jnp.bfloat16)
    return (hidden_out, normed)
```

```python
import math
import numpy as np
import jax
import jax.numpy as jnp
from jax import lax
from jax.experimental import pallas as pl
from jax.experimental.pallas import tpu as pltpu
import ml_dtypes
from jax.sharding import PartitionSpec as P

F32 = jnp.float32
BF16 = jnp.bfloat16
ROWS = 33
SLOTS = 40


def make_tables():
    d = np.arange(128)
    ang = -2.0 * np.pi * ((d[:, None] * d[None, :]) % 128) / 128
    fr, fi = np.cos(ang), np.sin(ang)
    u = np.block([[fr, -fi], [fi, fr]])
    tables = np.stack([u, u.T]).astype(ml_dtypes.bfloat16)
    ang = -2.0 * np.pi * (d[:, None] * d[None, :]) / 16384
    t0 = np.stack([np.cos(ang), np.sin(ang)]).astype(np.float32)
    place = np.arange(16384).reshape(128, 128)
    ang = -2.0 * np.pi * (np.arange(ROWS)[:, None, None] * place[None]) / 1048576
    w1 = np.stack([np.cos(ang), np.sin(ang)], axis=1).astype(np.float32)
    pick = np.zeros((2, 2, SLOTS, 128))
    perm = np.zeros((2, 2, 64, 2, 2, 128))
    for lo in range(2):
        for k1 in range(ROWS):
            alone = k1 in (0, 32)
            pick[0, lo, k1, lo * 64 + k1] = 2.0 ** -20 if alone else 2.0 ** -21
            if not alone:
                pick[1, lo, k1, lo * 64 + 64 - k1] = 2.0 ** -21
        for hi in range(64):
            k2 = 2 * hi + lo
            for part in range(2):
                perm[0, lo, hi, part, part, k2] = 1.0
                perm[1, lo, hi, part, part, 127 - k2] = 1.0 - 2.0 * part
    pick = pick.reshape(4 * SLOTS, 128).astype(ml_dtypes.bfloat16)
    perm = perm.reshape(512, 256).astype(ml_dtypes.bfloat16)
    return tables, t0, w1, pick, perm


def times(a, b, conj=False):
    if conj:
        return (a[0] * b[0] + a[1] * b[1], a[1] * b[0] - a[0] * b[1])
    return (a[0] * b[0] - a[1] * b[1], a[0] * b[1] + a[1] * b[0])


def turn(z, k, n, orient):
    re, im = z
    if k == 0:
        return z
    if 4 * k == n:
        if im is None:
            return (None, re if orient > 0 else -re)
        return (-im, re) if orient > 0 else (im, -re)
    c = math.cos(2.0 * math.pi * k / n)
    s = orient * math.sin(2.0 * math.pi * k / n)
    if im is None:
        return (re * c, re * s)
    if 8 * k == n:
        if orient > 0:
            return ((re - im) * c, (re + im) * c)
        return ((re + im) * c, (im - re) * c)
    return (re * c - im * s, re * s + im * c)


def plus(a, b):
    if a is None:
        return b
    if b is None:
        return a
    return a + b


def minus(a, b):
    if b is None:
        return a
    if a is None:
        return -b
    return a - b


def real_forward(vals, n):
    if n == 2:
        return [(vals[0], None), (vals[0], None)]
    even = real_forward(vals[0::2], n // 2)
    odd = real_forward(vals[1::2], n // 2)
    out = [None] * (n // 2 + 1)
    for k in range(n // 4 + 1):
        t = turn(odd[k], k, n, -1)
        e = even[k]
        out[k] = (plus(e[0], t[0]), plus(e[1], t[1]))
        if n // 2 - k != k:
            out[n // 2 - k] = (minus(e[0], t[0]), minus(t[1], e[1]))
    return out


def real_inverse(bins, n):
    if n == 2:
        return [bins[0][0] + bins[1][0]]
    even, odd = [], []
    for k in range(n // 4 + 1):
        a, b = bins[k], bins[n // 2 - k]
        even.append((plus(a[0], b[0]), minus(a[1], b[1])))
        t = (minus(a[0], b[0]), plus(a[1], b[1]))
        if k == n // 4:
            even[-1] = (a[0] + a[0], None)
            t = (None, a[1] + a[1])
            odd.append(turn_imag(t[1]))
        else:
            odd.append(turn(t, k, n, 1))
    first = real_inverse(even, n // 2)
    second = real_inverse(odd, n // 2)
    out = [None] * (n // 2)
    out[0::2] = first
    out[1::2] = second
    return out


def turn_imag(im):
    return (-im, None)


def filter_step(pairs_at, h_at, sh, pick, perm, direct):
    pieces = []
    for a, b in pairs_at:
        got = {}
        for name, k3 in (("a", a), ("b", b)):
            got[name] = lax.dot_general(
                pick, h_at(k3), (((1,), (1,)), ((), ())), preferred_element_type=F32
            ).astype(BF16)
        for mine, other in (("a", "b"), ("b", "a")):
            own, mirror = got[mine], got[other]
            pieces.append(
                jnp.concatenate(
                    [
                        own[0:SLOTS],
                        own[SLOTS : 2 * SLOTS],
                        mirror[2 * SLOTS : 3 * SLOTS],
                        mirror[3 * SLOTS : 4 * SLOTS],
                    ],
                    axis=1,
                )
            )
    joined = jnp.concatenate(pieces, axis=0)
    z = jnp.dot(joined, perm, preferred_element_type=F32)
    i = 0
    for a, b in pairs_at:
        for k3 in (a, b):
            zz = z[i * SLOTS : (i + 1) * SLOTS]
            sh[pl.ds(k3, SLOTS, stride=256), :] = zz[:, :128] + direct
            sh[pl.ds(128 + k3, SLOTS, stride=256), :] = zz[:, 128:]
            i += 1


def filter_prep(h_ref, sh, hs, pick_ref, perm_ref, direct, unroll=4):
    pick = pick_ref[...]
    perm = perm_ref[...]

    def h_at(k3):
        return h_ref[pl.ds(pl.multiple_of(k3 * 128, 128), 128), :]

    def step(i, c):
        filter_step(
            [(i * unroll + j, 127 - (i * unroll + j)) for j in range(unroll)],
            h_at, sh, pick, perm, direct,
        )
        return c

    lax.fori_loop(0, 64 // unroll, step, 0)

    def turn_over(i, c):
        for part in range(2):
            row = pl.multiple_of(i * 256 + part * 128, 128)
            hs[i, part] = sh[pl.ds(row, 128), :].T
        return c

    lax.fori_loop(0, ROWS, turn_over, 0)


def stage_one(load, a_ref, w1_ref, row, height=16):
    bins = real_forward([load(s) for s in range(32)], 64)
    for k1 in range(ROWS):
        re, im = bins[k1]
        if k1 == 0:
            im = jnp.zeros_like(re)
        else:
            wr = w1_ref[k1, 0, pl.ds(row, height), :]
            wi = w1_ref[k1, 1, pl.ds(row, height), :]
            if im is None:
                re, im = re * wr, re * wi
            else:
                re, im = times((re, im), (wr, wi))
        a_ref[k1, pl.ds(row, height), :] = re.astype(BF16)
        a_ref[k1, pl.ds(128 + row, height), :] = im.astype(BF16)


def middle(rows, a_ref, g_ref, hs, u, v, t0_ref):
    tr, ti = t0_ref[0], t0_ref[1]
    packed = jnp.concatenate([a_ref[k] for k in rows], axis=1)
    b = jnp.dot(u, packed, preferred_element_type=F32)
    lines = []
    for i, k in enumerate(rows):
        br, bi = b[:128, i * 128 : (i + 1) * 128], b[128:, i * 128 : (i + 1) * 128]
        re, im = times((br, bi), (tr, ti))
        lines.append(jnp.concatenate([re.astype(BF16), im.astype(BF16)], axis=1))
    c = jnp.dot(jnp.concatenate(lines, axis=0), v, preferred_element_type=F32)
    lines = []
    for i, k in enumerate(rows):
        cc = c[i * 128 : (i + 1) * 128]
        re, im = times((cc[:, :128], cc[:, 128:]), (hs[k, 0], hs[k, 1]))
        lines.append(jnp.concatenate([re.astype(BF16), im.astype(BF16)], axis=1))
    e = jnp.dot(jnp.concatenate(lines, axis=0), u, preferred_element_type=F32)
    cols = []
    for i, k in enumerate(rows):
        ee = e[i * 128 : (i + 1) * 128]
        re, im = times((ee[:, :128], ee[:, 128:]), (tr, ti), conj=True)
        cols.append(jnp.concatenate([re.astype(BF16), im.astype(BF16)], axis=0))
    g = jnp.dot(v, jnp.concatenate(cols, axis=1), preferred_element_type=F32)
    for i, k in enumerate(rows):
        g_ref[k] = g[:, i * 128 : (i + 1) * 128]


def all_middle(a_ref, g_ref, hs, uv_ref, t0_ref):
    u, v = uv_ref[0], uv_ref[1]

    def step(i, c):
        middle([2 * i, 2 * i + 1], a_ref, g_ref, hs, u, v, t0_ref)
        return c

    lax.fori_loop(0, 16, step, 0, unroll=4)
    middle([32], a_ref, g_ref, hs, u, v, t0_ref)


def stage_last(g_ref, w1_ref, row, height=16):
    bins = []
    for k1 in range(ROWS):
        re = g_ref[k1, pl.ds(row, height), :]
        im = g_ref[k1, pl.ds(128 + row, height), :]
        if k1 == 0:
            bins.append((re, None))
            continue
        wr = w1_ref[k1, 0, pl.ds(row, height), :]
        wi = w1_ref[k1, 1, pl.ds(row, height), :]
        if k1 == 32:
            bins.append((re * wr + im * wi, None))
        else:
            bins.append(times((re, im), (wr, wi), conj=True))
    return real_inverse(bins, 64)


SEQ = 32
CHAN = 8
SLAB = 16384
CHUNKS = 4
PC = 128 // CHUNKS
LANES = PC * 128
TILES = 4
MESH = pl.DeviceIdType.MESH


def hop(i):
    return lax.rem(i * 11, SEQ)


def fused(
    streams, wts, skip, h2, residual, gain, uv_in, t0_in, w1_in, pick_in, perm_in,
    out_h, out_n,
    st, flat, sb, xb, hv, sh, hs, a, g, uv, t0, w1, pick, perm, yb, rb,
    gate, res, hb, nb, sqp, sqa, rs, wb,
    load_sem, halo_sem, x_send, x_recv, y_send, y_recv, s_send, s_recv, o_sem,
):
    me = lax.axis_index("seq")
    mc = lax.axis_index("chan")

    loads = [
        pltpu.make_async_copy(
            streams.at[pl.ds(1, 2)], st.at[pl.ds(1, 2), :, pl.ds(128, SLAB)], load_sem.at[0]
        ),
        pltpu.make_async_copy(h2, hv, load_sem.at[1]),
        pltpu.make_async_copy(pick_in, pick, load_sem.at[2]),
        pltpu.make_async_copy(perm_in, perm, load_sem.at[3]),
        pltpu.make_async_copy(
            streams.at[pl.ds(0, 1)], st.at[pl.ds(0, 1), :, pl.ds(128, SLAB)], load_sem.at[4]
        ),
        pltpu.make_async_copy(w1_in, w1, load_sem.at[5]),
        pltpu.make_async_copy(uv_in, uv, load_sem.at[6]),
        pltpu.make_async_copy(t0_in, t0, load_sem.at[7]),
        pltpu.make_async_copy(residual, res, load_sem.at[8]),
    ]
    for copy in loads:
        copy.start()

    barrier = pltpu.get_barrier_semaphore()

    def greet_seq(i, c):
        pl.semaphore_signal(
            barrier, inc=1, device_id={"seq": lax.rem(me + i, SEQ)}, device_id_type=MESH
        )
        return c

    def greet_chan(i, c):
        pl.semaphore_signal(
            barrier, inc=1, device_id={"chan": lax.rem(mc + i, CHAN)}, device_id_type=MESH
        )
        return c

    lax.fori_loop(1, SEQ, greet_seq, 0)
    lax.fori_loop(1, CHAN, greet_chan, 0)

    eye = lax.broadcasted_iota(jnp.int32, (32, 32), 0) == lax.broadcasted_iota(
        jnp.int32, (32, 32), 1
    )

    def spread(row):
        column = jnp.sum(jnp.where(eye, row, 0.0), axis=1, keepdims=True)
        return jnp.broadcast_to(column, (32, 128))

    for stream in range(3):
        for tap in range(3):
            wb[stream * 3 + tap] = spread(wts[stream, pl.ds(tap, 1), :])
    wb[9] = spread(gain[...])

    pl.semaphore_wait(barrier, SEQ + CHAN - 2)

    halo = pltpu.make_async_remote_copy(
        src_ref=streams.at[:, :, pl.ds(SLAB - 128, 128)],
        dst_ref=st.at[:, :, pl.ds(0, 128)],
        send_sem=halo_sem.at[0],
        recv_sem=halo_sem.at[1],
        device_id={"seq": lax.rem(me + 1, SEQ)},
        device_id_type=MESH,
    )
    halo.start()

    lane = lax.broadcasted_iota(jnp.int32, (32, 128), 1)

    def short_conv(stream, first):
        cur = [
            st[stream, :, pl.ds(pl.multiple_of((first + i) * 128, 128), 128)].astype(F32)
            for i in range(TILES + 1)
        ]
        one = [pltpu.roll(t, 1, 1) for t in cur]
        two = [pltpu.roll(t, 2, 1) for t in cur]
        out = []
        for i in range(1, TILES + 1):
            back1 = jnp.where(lane < 1, one[i - 1], one[i])
            back2 = jnp.where(lane < 2, two[i - 1], two[i])
            out.append(
                wb[stream * 3] * cur[i] + wb[stream * 3 + 1] * back1 + wb[stream * 3 + 2] * back2
            )
        return out

    def gate_in(i, c):
        first = i * TILES
        one, two = short_conv(1, first), short_conv(2, first)
        for k in range(TILES):
            flat[pl.ds(pl.multiple_of((first + k) * 32, 32), 32), :] = one[k] * two[k]
        return c

    def send_chunk(j):
        lax.fori_loop(j * (PC // TILES), (j + 1) * (PC // TILES), gate_in, 0)

        def one_row(c):
            return flat[pl.ds(j * (PC * 32) + c, PC, stride=32), :].astype(BF16)

        rows = pl.ds(pl.multiple_of(j * PC, PC), PC)

        def send(i, c):
            peer = lax.rem(me + hop(i), SEQ)
            sb[peer, rows, :] = one_row(peer)
            pltpu.make_async_remote_copy(
                src_ref=sb.at[peer, rows],
                dst_ref=xb.at[j, me],
                send_sem=x_send.at[j],
                recv_sem=x_recv.at[j],
                device_id={"seq": peer},
                device_id_type=MESH,
            ).start()
            return c

        lax.fori_loop(1, SEQ, send, 0)
        xb[j, me] = one_row(me)

    loads[0].wait()

    def send_later(i, c):
        send_chunk(i + 1)
        return c

    lax.fori_loop(0, CHUNKS - 1, send_later, 0)
    loads[4].wait()
    halo.wait()
    st[:, :, pl.ds(0, 128)] = jnp.where(me > 0, st[:, :, pl.ds(0, 128)], jnp.zeros((3, 32, 128), BF16))
    send_chunk(0)

    for i in (1, 2, 3):
        loads[i].wait()
    filter_prep(hv, sh, hs, pick, perm, skip[me] * 2.0**-20)

    def gate_tiles(i, c):
        first = i * TILES
        vals = short_conv(0, first)
        for k in range(TILES):
            gate[:, pl.ds(pl.multiple_of((first + k) * 128, 128), 128)] = vals[k].astype(BF16)
        return c

    lax.fori_loop(0, 128 // TILES, gate_tiles, 0)
    for i in (5, 6, 7, 8):
        loads[i].wait()

    def all_of(buf, j, sem):
        return pltpu.make_async_copy(
            buf.at[j, pl.ds(0, SEQ - 1)], buf.at[j, pl.ds(0, SEQ - 1)], sem.at[j]
        )

    def first_stage(i, c):
        j = lax.rem(i + 1, CHUNKS)
        all_of(xb, j, x_recv).wait()

        def part(k, c):
            r = pl.multiple_of(k * 16, 16)
            stage_one(
                lambda s: xb[j, s, pl.ds(r, 16), :].astype(F32),
                a, w1, pl.multiple_of(j * PC + k * 16, 16),
            )
            return c

        lax.fori_loop(0, PC // 16, part, 0)
        return c

    lax.fori_loop(0, CHUNKS, first_stage, 0)
    all_middle(a, g, hs, uv, t0)

    def last_stage(j, c):
        def part(k, c):
            ys = stage_last(g, w1, pl.multiple_of(j * PC + k * 16, 16))
            for s in range(SEQ):
                yb[j, s, pl.ds(pl.multiple_of(k * 16, 16), 16), :] = ys[s].astype(BF16)
            return c

        lax.fori_loop(0, PC // 16, part, 0)

        def send(i, c):
            peer = lax.rem(me + hop(i), SEQ)
            pltpu.make_async_remote_copy(
                src_ref=yb.at[j, peer],
                dst_ref=rb.at[j, me],
                send_sem=y_send.at[j],
                recv_sem=y_recv.at[j],
                device_id={"seq": peer},
                device_id_type=MESH,
            ).start()
            return c

        lax.fori_loop(1, SEQ, send, 0)
        rb[j, me] = yb[j, me]
        return c

    lax.fori_loop(0, CHUNKS, last_stage, 0)

    def combine(j, c):
        all_of(rb, j, y_recv).wait()

        def spread_row(ch, c):
            flat[pl.ds(j * (PC * 32) + ch, PC, stride=32), :] = rb[j, ch].astype(F32)
            return c

        lax.fori_loop(0, 32, spread_row, 0, unroll=4)

        def tile(r, c):
            p = j * PC + r
            cols = pl.ds(pl.multiple_of(p * 128, 128), 128)
            long_out = flat[pl.ds(pl.multiple_of(p * 32, 32), 32), :]
            hidden = (res[:, cols].astype(F32) + gate[:, cols].astype(F32) * long_out).astype(BF16)
            hb[:, cols] = hidden
            wide = hidden.astype(F32)
            sqp[j, pl.ds(r, 1), :] = jnp.sum(wide * wide, axis=0, keepdims=True)
            return c

        lax.fori_loop(0, PC, tile, 0, unroll=4)

        def send(i, c):
            pltpu.make_async_remote_copy(
                src_ref=sqp.at[j],
                dst_ref=sqa.at[j, mc],
                send_sem=s_send.at[j],
                recv_sem=s_recv.at[j],
                device_id={"chan": lax.rem(mc + i, CHAN)},
                device_id_type=MESH,
            ).start()
            return c

        lax.fori_loop(1, CHAN, send, 0)
        sqa[j, mc] = sqp[j]
        cols = pl.ds(pl.multiple_of(j * LANES, LANES), LANES)
        pltpu.make_async_copy(hb.at[:, cols], out_h.at[:, cols], o_sem.at[0, j]).start()
        return c

    def norm(j, c):
        pltpu.make_async_copy(
            sqa.at[j, pl.ds(0, CHAN - 1)], sqa.at[j, pl.ds(0, CHAN - 1)], s_recv.at[j]
        ).wait()
        total = sqa[j, 0]
        for k in range(1, CHAN):
            total = total + sqa[j, k]
        rs[...] = lax.rsqrt(total * (1.0 / (32 * CHAN)) + 1e-06)

        def tile(r, c):
            cols = pl.ds(pl.multiple_of((j * PC + r) * 128, 128), 128)
            scale = wb[9] * rs[pl.ds(r, 1), :]
            nb[:, cols] = (hb[:, cols].astype(F32) * scale).astype(BF16)
            return c

        lax.fori_loop(0, PC, tile, 0, unroll=4)
        cols = pl.ds(pl.multiple_of(j * LANES, LANES), LANES)
        pltpu.make_async_copy(nb.at[:, cols], out_n.at[:, cols], o_sem.at[1, j]).start()
        return c

    combine(0, 0)

    def both(j, c):
        combine(j, c)
        return norm(j - 1, c)

    lax.fori_loop(1, CHUNKS, both, 0)
    norm(CHUNKS - 1, 0)

    def finish(j, c):
        all_of(xb, j, x_send).wait()
        all_of(rb, j, y_send).wait()
        pltpu.make_async_copy(
            sqa.at[j, pl.ds(0, CHAN - 1)], sqa.at[j, pl.ds(0, CHAN - 1)], s_send.at[j]
        ).wait()
        cols = pl.ds(pl.multiple_of(j * LANES, LANES), LANES)
        pltpu.make_async_copy(hb.at[:, cols], out_h.at[:, cols], o_sem.at[0, j]).wait()
        pltpu.make_async_copy(nb.at[:, cols], out_n.at[:, cols], o_sem.at[1, j]).wait()
        return c

    lax.fori_loop(0, CHUNKS, finish, 0)


def per_device(streams, conv_weights, skip, filter_spec, residual, gain):
    tables = [jnp.asarray(t) for t in make_tables()]
    h2 = filter_spec.reshape(2, 8192, 128).transpose(1, 0, 2).reshape(16384, 128)
    far = pl.BlockSpec(memory_space=pl.ANY)
    near = pl.BlockSpec(memory_space=pltpu.VMEM)
    slab = (32, SLAB)
    dma = pltpu.SemaphoreType.DMA
    vmem = pltpu.VMEM
    return pl.pallas_call(
        fused,
        out_shape=[jax.ShapeDtypeStruct(slab, BF16)] * 2,
        in_specs=[far, near, pl.BlockSpec(memory_space=pltpu.SMEM), far, far, near] + [far] * 5,
        out_specs=[far, far],
        scratch_shapes=[
            vmem((3, 32, 128 + SLAB), BF16),
            vmem((4096, 128), F32),
            vmem((32, 128, 128), BF16),
            vmem((CHUNKS, 32, PC, 128), BF16),
            vmem((16384, 128), BF16),
            vmem((SLOTS * 256, 128), F32),
            vmem((ROWS, 2, 128, 128), F32),
            vmem((ROWS, 256, 128), BF16),
            vmem((ROWS, 256, 128), F32),
            vmem((2, 256, 256), BF16),
            vmem((2, 128, 128), F32),
            vmem((ROWS, 2, 128, 128), F32),
            vmem((4 * SLOTS, 128), BF16),
            vmem((512, 256), BF16),
            vmem((CHUNKS, 32, PC, 128), BF16),
            vmem((CHUNKS, 32, PC, 128), BF16),
            vmem(slab, BF16),
            vmem(slab, BF16),
            vmem(slab, BF16),
            vmem(slab, BF16),
            vmem((CHUNKS, PC, 128), F32),
            vmem((CHUNKS, CHAN, PC, 128), F32),
            vmem((PC, 128), F32),
            vmem((10, 32, 128), F32),
            dma((9,)),
            dma((2,)),
            dma((CHUNKS,)),
            dma((CHUNKS,)),
            dma((CHUNKS,)),
            dma((CHUNKS,)),
            dma((CHUNKS,)),
            dma((CHUNKS,)),
            dma((2, CHUNKS)),
        ],
        compiler_params=pltpu.CompilerParams(
            collective_id=0, has_side_effects=True, vmem_limit_bytes=60 * 2**20
        ),
        cost_estimate=pl.CostEstimate(
            flops=8 * 10**9, bytes_accessed=20 * 2**20, transcendentals=0
        ),
    )(
        streams,
        conv_weights.transpose(0, 2, 1),
        skip,
        h2,
        residual,
        gain.reshape(1, 32),
        *tables,
    )


def solution(mesh):
    in_specs = (
        P(None, "chan", "seq"),
        P(None, "chan", None),
        P("chan"),
        P("chan", "seq", None, None),
        P("chan", "seq"),
        P("chan"),
    )
    out_specs = [P("chan", "seq"), P("chan", "seq")]
    return jax.shard_map(
        lambda *args: tuple(per_device(*args)),
        mesh=mesh,
        in_specs=in_specs,
        out_specs=tuple(out_specs),
        check_vma=False,
    )
```

```python
import math
import numpy as np
import jax
import jax.numpy as jnp
from jax import lax
from jax.experimental import pallas as pl
from jax.experimental.pallas import tpu as pltpu
import ml_dtypes
from jax.sharding import PartitionSpec as P

F32 = jnp.float32
BF16 = jnp.bfloat16
ROWS = 33
SLOTS = 40


def make_tables():
    d = np.arange(128)
    ang = -2.0 * np.pi * ((d[:, None] * d[None, :]) % 128) / 128
    fr, fi = np.cos(ang), np.sin(ang)
    u = np.block([[fr, -fi], [fi, fr]])
    tables = np.stack([u, u.T]).astype(ml_dtypes.bfloat16)
    ang = -2.0 * np.pi * (d[:, None] * d[None, :]) / 16384
    t0 = np.stack([np.cos(ang), np.sin(ang)]).astype(np.float32)
    place = np.arange(16384).reshape(128, 128)
    ang = -2.0 * np.pi * (np.arange(ROWS)[:, None, None] * place[None]) / 1048576
    w1 = np.stack([np.cos(ang), np.sin(ang)], axis=1).astype(np.float32)
    pick = np.zeros((2, 2, SLOTS, 128))
    perm = np.zeros((2, 2, 64, 2, 2, 128))
    for lo in range(2):
        for k1 in range(ROWS):
            alone = k1 in (0, 32)
            pick[0, lo, k1, lo * 64 + k1] = 2.0 ** -20 if alone else 2.0 ** -21
            if not alone:
                pick[1, lo, k1, lo * 64 + 64 - k1] = 2.0 ** -21
        for hi in range(64):
            k2 = 2 * hi + lo
            for part in range(2):
                perm[0, lo, hi, part, part, k2] = 1.0
                perm[1, lo, hi, part, part, 127 - k2] = 1.0 - 2.0 * part
    pick = pick.reshape(4 * SLOTS, 128).astype(ml_dtypes.bfloat16)
    perm = perm.reshape(512, 256).astype(ml_dtypes.bfloat16)
    return tables, t0, w1, pick, perm


def times(a, b, conj=False):
    if conj:
        return (a[0] * b[0] + a[1] * b[1], a[1] * b[0] - a[0] * b[1])
    return (a[0] * b[0] - a[1] * b[1], a[0] * b[1] + a[1] * b[0])


def turn(z, k, n, orient):
    re, im = z
    if k == 0:
        return z
    if 4 * k == n:
        if im is None:
            return (None, re if orient > 0 else -re)
        return (-im, re) if orient > 0 else (im, -re)
    c = math.cos(2.0 * math.pi * k / n)
    s = orient * math.sin(2.0 * math.pi * k / n)
    if im is None:
        return (re * c, re * s)
    if 8 * k == n:
        if orient > 0:
            return ((re - im) * c, (re + im) * c)
        return ((re + im) * c, (im - re) * c)
    return (re * c - im * s, re * s + im * c)


def plus(a, b):
    if a is None:
        return b
    if b is None:
        return a
    return a + b


def minus(a, b):
    if b is None:
        return a
    if a is None:
        return -b
    return a - b


def real_forward(vals, n):
    if n == 2:
        return [(vals[0], None), (vals[0], None)]
    even = real_forward(vals[0::2], n // 2)
    odd = real_forward(vals[1::2], n // 2)
    out = [None] * (n // 2 + 1)
    for k in range(n // 4 + 1):
        t = turn(odd[k], k, n, -1)
        e = even[k]
        out[k] = (plus(e[0], t[0]), plus(e[1], t[1]))
        if n // 2 - k != k:
            out[n // 2 - k] = (minus(e[0], t[0]), minus(t[1], e[1]))
    return out


def real_inverse(bins, n):
    if n == 2:
        return [bins[0][0] + bins[1][0]]
    even, odd = [], []
    for k in range(n // 4 + 1):
        a, b = bins[k], bins[n // 2 - k]
        even.append((plus(a[0], b[0]), minus(a[1], b[1])))
        t = (minus(a[0], b[0]), plus(a[1], b[1]))
        if k == n // 4:
            even[-1] = (a[0] + a[0], None)
            t = (None, a[1] + a[1])
            odd.append(turn_imag(t[1]))
        else:
            odd.append(turn(t, k, n, 1))
    first = real_inverse(even, n // 2)
    second = real_inverse(odd, n // 2)
    out = [None] * (n // 2)
    out[0::2] = first
    out[1::2] = second
    return out


def turn_imag(im):
    return (-im, None)


def filter_step(pairs_at, h_at, sh, pick, perm, direct):
    pieces = []
    for a, b in pairs_at:
        got = {}
        for name, k3 in (("a", a), ("b", b)):
            got[name] = lax.dot_general(
                pick, h_at(k3), (((1,), (1,)), ((), ())), preferred_element_type=F32
            ).astype(BF16)
        for mine, other in (("a", "b"), ("b", "a")):
            own, mirror = got[mine], got[other]
            pieces.append(
                jnp.concatenate(
                    [
                        own[0:SLOTS],
                        own[SLOTS : 2 * SLOTS],
                        mirror[2 * SLOTS : 3 * SLOTS],
                        mirror[3 * SLOTS : 4 * SLOTS],
                    ],
                    axis=1,
                )
            )
    joined = jnp.concatenate(pieces, axis=0)
    z = jnp.dot(joined, perm, preferred_element_type=F32)
    i = 0
    for a, b in pairs_at:
        for k3 in (a, b):
            zz = z[i * SLOTS : (i + 1) * SLOTS]
            sh[pl.ds(k3, SLOTS, stride=256), :] = zz[:, :128] + direct
            sh[pl.ds(128 + k3, SLOTS, stride=256), :] = zz[:, 128:]
            i += 1


def filter_prep(h_ref, sh, hs, pick_ref, perm_ref, direct, unroll=4):
    pick = pick_ref[...]
    perm = perm_ref[...]

    def h_at(k3):
        return h_ref[pl.ds(pl.multiple_of(k3 * 128, 128), 128), :]

    def step(i, c):
        filter_step(
            [(i * unroll + j, 127 - (i * unroll + j)) for j in range(unroll)],
            h_at, sh, pick, perm, direct,
        )
        return c

    lax.fori_loop(0, 64 // unroll, step, 0)

    def turn_over(i, c):
        for part in range(2):
            row = pl.multiple_of(i * 256 + part * 128, 128)
            hs[i, part] = sh[pl.ds(row, 128), :].T
        return c

    lax.fori_loop(0, ROWS, turn_over, 0)


def stage_one(load, a_ref, w1_ref, row, height=16):
    bins = real_forward([load(s) for s in range(32)], 64)
    for k1 in range(ROWS):
        re, im = bins[k1]
        if k1 == 0:
            im = jnp.zeros_like(re)
        else:
            wr = w1_ref[k1, 0, pl.ds(row, height), :]
            wi = w1_ref[k1, 1, pl.ds(row, height), :]
            if im is None:
                re, im = re * wr, re * wi
            else:
                re, im = times((re, im), (wr, wi))
        a_ref[k1, pl.ds(row, height), :] = re.astype(BF16)
        a_ref[k1, pl.ds(128 + row, height), :] = im.astype(BF16)


def middle(groups, a_ref, g_ref, hs, u, v, t0_ref):
    tr, ti = t0_ref[0], t0_ref[1]

    def along_lanes(re, im):
        return jnp.concatenate([re.astype(BF16), im.astype(BF16)], axis=1)

    b = [
        jnp.dot(
            u, jnp.concatenate([a_ref[k] for k in rows], axis=1), preferred_element_type=F32
        )
        for rows in groups
    ]
    lines = []
    for rows, x in zip(groups, b):
        lines.append(
            jnp.concatenate(
                [
                    along_lanes(
                        *times(
                            (x[:128, i * 128 : (i + 1) * 128], x[128:, i * 128 : (i + 1) * 128]),
                            (tr, ti),
                        )
                    )
                    for i in range(len(rows))
                ],
                axis=0,
            )
        )
    c = [jnp.dot(x, v, preferred_element_type=F32) for x in lines]
    lines = []
    for rows, x in zip(groups, c):
        lines.append(
            jnp.concatenate(
                [
                    along_lanes(
                        *times(
                            (x[i * 128 : (i + 1) * 128, :128], x[i * 128 : (i + 1) * 128, 128:]),
                            (hs[k, 0], hs[k, 1]),
                        )
                    )
                    for i, k in enumerate(rows)
                ],
                axis=0,
            )
        )
    e = [jnp.dot(x, u, preferred_element_type=F32) for x in lines]
    lines = []
    for rows, x in zip(groups, e):
        cols = []
        for i in range(len(rows)):
            re, im = times(
                (x[i * 128 : (i + 1) * 128, :128], x[i * 128 : (i + 1) * 128, 128:]),
                (tr, ti),
                conj=True,
            )
            cols.append(jnp.concatenate([re.astype(BF16), im.astype(BF16)], axis=0))
        lines.append(jnp.concatenate(cols, axis=1))
    g = [jnp.dot(v, x, preferred_element_type=F32) for x in lines]
    for rows, x in zip(groups, g):
        for i, k in enumerate(rows):
            g_ref[k] = x[:, i * 128 : (i + 1) * 128]


def all_middle(a_ref, g_ref, hs, uv_ref, t0_ref):
    u, v = uv_ref[0], uv_ref[1]
    pairs = [[2 * i, 2 * i + 1] for i in range(16)]
    middle(pairs[:8], a_ref, g_ref, hs, u, v, t0_ref)
    middle(pairs[8:] + [[32]], a_ref, g_ref, hs, u, v, t0_ref)


def stage_last(g_ref, w1_ref, row, height=16):
    bins = []
    for k1 in range(ROWS):
        re = g_ref[k1, pl.ds(row, height), :]
        im = g_ref[k1, pl.ds(128 + row, height), :]
        if k1 == 0:
            bins.append((re, None))
            continue
        wr = w1_ref[k1, 0, pl.ds(row, height), :]
        wi = w1_ref[k1, 1, pl.ds(row, height), :]
        if k1 == 32:
            bins.append((re * wr + im * wi, None))
        else:
            bins.append(times((re, im), (wr, wi), conj=True))
    return real_inverse(bins, 64)


SEQ = 32
CHAN = 8
SLAB = 16384
TILES = 4
MESH = pl.DeviceIdType.MESH
THERE = [(0, 32, 32), (1, 64, 32), (2, 96, 32), (3, 16, 16), (4, 0, 16)]
BACK = [(0, 0, 16), (1, 16, 32), (2, 48, 32), (3, 80, 32), (4, 112, 16)]


def each_peer(fn, count, per):
    def step(i, c):
        for k in range(per):
            fn(i * per + k + 1)
        return c

    whole = (count - 1) // per
    lax.fori_loop(0, whole, step, 0)
    for i in range(whole * per + 1, count):
        fn(i)


def fused(
    streams, wts, skip, h2, residual, gain, uv_in, t0_in, w1_in, pick_in, perm_in,
    out_h, out_r,
    st, flat, sb, xb, hv, sh, hs, a, g, uv, t0, w1, pick, perm, yb, rb,
    gate, res, hb, sqp, sqa, rs, wb,
    load_sem, halo_sem, x_send, x_recv, y_send, y_recv, s_send, s_recv, o_sem,
):
    me = lax.axis_index("seq")
    mc = lax.axis_index("chan")

    def seq_peer(i):
        return lax.rem(me + i * 11, SEQ)

    def chan_peer(i):
        return lax.rem(mc + i, CHAN)

    loads = [
        pltpu.make_async_copy(
            streams.at[pl.ds(1, 2)], st.at[pl.ds(1, 2), :, pl.ds(128, SLAB)], load_sem.at[0]
        ),
        pltpu.make_async_copy(h2, hv, load_sem.at[1]),
        pltpu.make_async_copy(pick_in, pick, load_sem.at[2]),
        pltpu.make_async_copy(perm_in, perm, load_sem.at[3]),
        pltpu.make_async_copy(
            streams.at[pl.ds(0, 1)], st.at[pl.ds(0, 1), :, pl.ds(128, SLAB)], load_sem.at[4]
        ),
        pltpu.make_async_copy(w1_in, w1, load_sem.at[5]),
        pltpu.make_async_copy(uv_in, uv, load_sem.at[6]),
        pltpu.make_async_copy(t0_in, t0, load_sem.at[7]),
        pltpu.make_async_copy(residual, res, load_sem.at[8]),
    ]
    loads[0].start()

    barrier = pltpu.get_barrier_semaphore()

    def greet_seq(i):
        pl.semaphore_signal(
            barrier, inc=1, device_id={"seq": lax.rem(me + i, SEQ)}, device_id_type=MESH
        )

    def greet_chan(i):
        pl.semaphore_signal(barrier, inc=1, device_id={"chan": chan_peer(i)}, device_id_type=MESH)

    each_peer(greet_seq, SEQ, 5)
    each_peer(greet_chan, CHAN, 7)

    eye = lax.broadcasted_iota(jnp.int32, (32, 32), 0) == lax.broadcasted_iota(
        jnp.int32, (32, 32), 1
    )

    def spread(row):
        column = jnp.sum(jnp.where(eye, row, 0.0), axis=1, keepdims=True)
        return jnp.broadcast_to(column, (32, 128))

    for stream in range(3):
        for tap in range(3):
            wb[stream * 3 + tap] = spread(wts[stream, pl.ds(tap, 1), :])

    lane = lax.broadcasted_iota(jnp.int32, (32, 128), 1)

    def short_conv(stream, first):
        cur = [
            st[stream, :, pl.ds(pl.multiple_of((first + i) * 128, 128), 128)].astype(F32)
            for i in range(TILES + 1)
        ]
        one = [pltpu.roll(t, 1, 1) for t in cur]
        two = [pltpu.roll(t, 2, 1) for t in cur]
        out = []
        for i in range(1, TILES + 1):
            back1 = jnp.where(lane < 1, one[i - 1], one[i])
            back2 = jnp.where(lane < 2, two[i - 1], two[i])
            out.append(
                wb[stream * 3] * cur[i] + wb[stream * 3 + 1] * back1 + wb[stream * 3 + 2] * back2
            )
        return out

    def gate_rows(start, rows):
        def gate_in(i, c):
            first = start + i * TILES
            one, two = short_conv(1, first), short_conv(2, first)
            for k in range(TILES):
                flat[pl.ds(pl.multiple_of((first + k) * 32, 32), 32), :] = one[k] * two[k]
            return c

        lax.fori_loop(0, rows // TILES, gate_in, 0)

    def one_row(start, rows, c):
        return flat[pl.ds(start * 32 + c, rows, stride=32), :].astype(BF16)

    def send_rows(n, start, rows):
        span = pl.ds(pl.multiple_of(start, 16), rows)

        def send(i):
            peer = seq_peer(i)
            sb[peer, span, :] = one_row(start, rows, peer)
            pltpu.make_async_remote_copy(
                src_ref=sb.at[peer, span],
                dst_ref=xb.at[me, span],
                send_sem=x_send.at[n],
                recv_sem=x_recv.at[n],
                device_id={"seq": peer},
                device_id_type=MESH,
            ).start()

        each_peer(send, SEQ, 3)
        xb[me, span, :] = one_row(start, rows, me)

    loads[0].wait()
    for i in range(1, 9):
        loads[i].start()
    gate_rows(32, 32)
    pl.semaphore_wait(barrier, SEQ + CHAN - 2)
    halo = pltpu.make_async_remote_copy(
        src_ref=streams.at[:, :, pl.ds(SLAB - 128, 128)],
        dst_ref=st.at[:, :, pl.ds(0, 128)],
        send_sem=halo_sem.at[0],
        recv_sem=halo_sem.at[1],
        device_id={"seq": lax.rem(me + 1, SEQ)},
        device_id_type=MESH,
    )
    halo.start()
    send_rows(0, 32, 32)

    def send_more(n, c):
        start = n * 32 + 32
        gate_rows(start, 32)
        send_rows(n, start, 32)
        return c

    lax.fori_loop(1, 3, send_more, 0)
    gate_rows(16, 16)
    send_rows(3, 16, 16)
    halo.wait()
    rim = st[:, :, pl.ds(0, 128)]
    st[:, :, pl.ds(0, 128)] = jnp.where(me > 0, rim, jnp.zeros_like(rim))
    gate_rows(0, 16)
    send_rows(4, 0, 16)

    for i in (1, 2, 3):
        loads[i].wait()
    filter_prep(hv, sh, hs, pick, perm, skip[me] * 2.0**-20)
    loads[4].wait()

    def gate_tiles(i, c):
        first = i * TILES
        vals = short_conv(0, first)
        for k in range(TILES):
            gate[:, pl.ds(pl.multiple_of((first + k) * 128, 128), 128)] = vals[k].astype(BF16)
        return c

    lax.fori_loop(0, 128 // TILES, gate_tiles, 0)
    for i in (5, 6, 7, 8):
        loads[i].wait()

    def all_of(buf, start, rows, sem):
        part = buf.at[pl.ds(0, SEQ - 1), pl.ds(pl.multiple_of(start, 16), rows)]
        return pltpu.make_async_copy(part, part, sem)

    def transform_rows(n, start, rows):
        all_of(xb, start, rows, x_recv.at[n]).wait()

        def part(k, c):
            r = pl.multiple_of(start + k * 16, 16)
            stage_one(lambda s: xb[s, pl.ds(r, 16), :].astype(F32), a, w1, r)
            return c

        lax.fori_loop(0, rows // 16, part, 0)

    def transform_more(n, c):
        transform_rows(n, n * 32 + 32, 32)
        return c

    def transform_last(n, c):
        transform_rows(n, (4 - n) * 16, 16)
        return c

    lax.fori_loop(0, 3, transform_more, 0)
    lax.fori_loop(3, 5, transform_last, 0)
    all_middle(a, g, hs, uv, t0)

    def back_rows(n, start, rows):
        def part(k, c):
            r = pl.multiple_of(start + k * 16, 16)
            ys = stage_last(g, w1, r)
            for s in range(SEQ):
                yb[s, pl.ds(r, 16), :] = ys[s].astype(BF16)
            return c

        lax.fori_loop(0, rows // 16, part, 0)
        span = pl.ds(pl.multiple_of(start, 16), rows)

        def send(i):
            peer = seq_peer(i)
            pltpu.make_async_remote_copy(
                src_ref=yb.at[peer, span],
                dst_ref=rb.at[me, span],
                send_sem=y_send.at[n],
                recv_sem=y_recv.at[n],
                device_id={"seq": peer},
                device_id_type=MESH,
            ).start()

        each_peer(send, SEQ, 5)
        rb[me, span, :] = yb[me, span, :]

    def back_more(n, c):
        back_rows(n, n * 32 - 16, 32)
        return c

    back_rows(0, 0, 16)
    lax.fori_loop(1, 4, back_more, 0)
    back_rows(4, 112, 16)

    def sums_of(start, rows, sem):
        part = sqa.at[pl.ds(0, CHAN - 1), pl.ds(pl.multiple_of(start, 16), rows)]
        return pltpu.make_async_copy(part, part, sem)

    def hidden_out(n, start, rows):
        cols = pl.ds(pl.multiple_of(start * 128, 128), rows * 128)
        return pltpu.make_async_copy(hb.at[:, cols], out_h.at[:, cols], o_sem.at[n])

    def combine(n, start, rows):
        all_of(rb, start, rows, y_recv.at[n]).wait()
        span = pl.ds(pl.multiple_of(start, 16), rows)

        def spread_row(ch, c):
            flat[pl.ds(start * 32 + ch, rows, stride=32), :] = rb[ch, span, :].astype(F32)
            return c

        lax.fori_loop(0, 32, spread_row, 0, unroll=8)

        def tile(r, c):
            p = start + r
            cols = pl.ds(pl.multiple_of(p * 128, 128), 128)
            long_out = flat[pl.ds(pl.multiple_of(p * 32, 32), 32), :]
            hidden = (res[:, cols].astype(F32) + gate[:, cols].astype(F32) * long_out).astype(BF16)
            hb[:, cols] = hidden
            wide = hidden.astype(F32)
            sqp[pl.ds(p, 1), :] = jnp.sum(wide * wide, axis=0, keepdims=True)
            return c

        lax.fori_loop(0, rows, tile, 0, unroll=8)

        def send(i):
            pltpu.make_async_remote_copy(
                src_ref=sqp.at[span],
                dst_ref=sqa.at[mc, span],
                send_sem=s_send.at[n],
                recv_sem=s_recv.at[n],
                device_id={"chan": chan_peer(i)},
                device_id_type=MESH,
            ).start()

        each_peer(send, CHAN, 7)
        sqa[mc, span, :] = sqp[span, :]
        hidden_out(n, start, rows).start()

    def norm(n, start, rows):
        sums_of(start, rows, s_recv.at[n]).wait()
        span = pl.ds(pl.multiple_of(start, 16), rows)
        total = sqa[0, span, :]
        for k in range(1, CHAN):
            total = total + sqa[k, span, :]
        rs[span, :] = lax.rsqrt(total * (1.0 / (32 * CHAN)) + 1e-06)

    def combine_more(n, c):
        combine(n, n * 32 - 16, 32)
        return c

    def norm_more(n, c):
        norm(n, n * 32 - 16, 32)
        return c

    combine(0, 0, 16)
    lax.fori_loop(1, 4, combine_more, 0)
    combine(4, 112, 16)
    norm(0, 0, 16)
    lax.fori_loop(1, 4, norm_more, 0)
    norm(4, 112, 16)
    scale_out = pltpu.make_async_copy(rs, out_r, o_sem.at[5])
    scale_out.start()
    for n, start, rows in THERE:
        all_of(xb, start, rows, x_send.at[n]).wait()
    for n, start, rows in BACK:
        all_of(rb, start, rows, y_send.at[n]).wait()
        sums_of(start, rows, s_send.at[n]).wait()
        hidden_out(n, start, rows).wait()
    scale_out.wait()


PARTS = 4


def finish(hidden, scale, gain, out_h, out_n, hb, nb, rs, gb, in_sem, out_sem):
    size = SLAB // PARTS

    def cols(j):
        return pl.ds(j * size, size)

    scale_in = pltpu.make_async_copy(scale, rs, in_sem.at[PARTS])
    scale_in.start()
    ins = [
        pltpu.make_async_copy(hidden.at[:, cols(j)], hb.at[:, cols(j)], in_sem.at[j])
        for j in range(PARTS)
    ]
    for copy in ins:
        copy.start()
    eye = lax.broadcasted_iota(jnp.int32, (32, 32), 0) == lax.broadcasted_iota(
        jnp.int32, (32, 32), 1
    )
    column = jnp.sum(jnp.where(eye, gain[...], 0.0), axis=1, keepdims=True)
    gb[...] = jnp.broadcast_to(column, (32, 128))
    scale_in.wait()
    outs = []
    for j in range(PARTS):
        ins[j].wait()
        outs.append(pltpu.make_async_copy(hb.at[:, cols(j)], out_h.at[:, cols(j)], out_sem.at[0, j]))
        outs[-1].start()

        def tile(r, c):
            p = j * (128 // PARTS) + r
            here = pl.ds(pl.multiple_of(p * 128, 128), 128)
            nb[:, here] = (hb[:, here].astype(F32) * (gb[...] * rs[pl.ds(p, 1), :])).astype(BF16)
            return c

        lax.fori_loop(0, 128 // PARTS, tile, 0, unroll=8)
        outs.append(pltpu.make_async_copy(nb.at[:, cols(j)], out_n.at[:, cols(j)], out_sem.at[1, j]))
        outs[-1].start()
    for copy in outs:
        copy.wait()


def per_device(streams, conv_weights, skip, filter_spec, residual, gain):
    tables = [jnp.asarray(t) for t in make_tables()]
    h2 = filter_spec.reshape(2, 8192, 128).transpose(1, 0, 2).reshape(16384, 128)
    far = pl.BlockSpec(memory_space=pl.ANY)
    near = pl.BlockSpec(memory_space=pltpu.VMEM)
    slab = (32, SLAB)
    dma = pltpu.SemaphoreType.DMA
    vmem = pltpu.VMEM
    line = gain.reshape(1, 32)
    hidden, scale = pl.pallas_call(
        fused,
        out_shape=[
            jax.ShapeDtypeStruct(slab, BF16),
            jax.ShapeDtypeStruct((128, 128), F32),
        ],
        in_specs=[far, near, pl.BlockSpec(memory_space=pltpu.SMEM), far, far, near] + [far] * 5,
        out_specs=[far, far],
        scratch_shapes=[
            vmem((3, 32, 128 + SLAB), BF16),
            vmem((4096, 128), F32),
            vmem((32, 128, 128), BF16),
            vmem((32, 128, 128), BF16),
            vmem((16384, 128), BF16),
            vmem((SLOTS * 256, 128), F32),
            vmem((ROWS, 2, 128, 128), F32),
            vmem((ROWS, 256, 128), BF16),
            vmem((ROWS, 256, 128), F32),
            vmem((2, 256, 256), BF16),
            vmem((2, 128, 128), F32),
            vmem((ROWS, 2, 128, 128), F32),
            vmem((4 * SLOTS, 128), BF16),
            vmem((512, 256), BF16),
            vmem((32, 128, 128), BF16),
            vmem((32, 128, 128), BF16),
            vmem(slab, BF16),
            vmem(slab, BF16),
            vmem(slab, BF16),
            vmem((128, 128), F32),
            vmem((CHAN, 128, 128), F32),
            vmem((128, 128), F32),
            vmem((9, 32, 128), F32),
            dma((9,)),
            dma((2,)),
            dma((5,)),
            dma((5,)),
            dma((5,)),
            dma((5,)),
            dma((5,)),
            dma((5,)),
            dma((6,)),
        ],
        compiler_params=pltpu.CompilerParams(
            collective_id=0, has_side_effects=True, vmem_limit_bytes=60 * 2**20
        ),
        cost_estimate=pl.CostEstimate(
            flops=8 * 10**9, bytes_accessed=20 * 2**20, transcendentals=0
        ),
    )(streams, conv_weights.transpose(0, 2, 1), skip, h2, residual, line, *tables)
    return pl.pallas_call(
        finish,
        out_shape=[jax.ShapeDtypeStruct(slab, BF16)] * 2,
        in_specs=[far, far, near],
        out_specs=[far, far],
        scratch_shapes=[
            vmem(slab, BF16),
            vmem(slab, BF16),
            vmem((128, 128), F32),
            vmem((32, 128), F32),
            dma((PARTS + 1,)),
            dma((2, PARTS)),
        ],
        compiler_params=pltpu.CompilerParams(vmem_limit_bytes=60 * 2**20),
        cost_estimate=pl.CostEstimate(
            flops=3 * 2**19, bytes_accessed=3 * 2**20, transcendentals=0
        ),
    )(hidden, scale, line)


def solution(mesh):
    in_specs = (
        P(None, "chan", "seq"),
        P(None, "chan", None),
        P("chan"),
        P("chan", "seq", None, None),
        P("chan", "seq"),
        P("chan"),
    )
    return jax.shard_map(
        lambda *args: tuple(per_device(*args)),
        mesh=mesh,
        in_specs=in_specs,
        out_specs=(P("chan", "seq"), P("chan", "seq")),
        check_vma=False,
    )
```

```python
import math
import numpy as np
import jax
import jax.numpy as jnp
from jax import lax
from jax.experimental import pallas as pl
from jax.experimental.pallas import tpu as pltpu
import ml_dtypes
from jax.sharding import PartitionSpec as P

F32 = jnp.float32
BF16 = jnp.bfloat16
ROWS = 33
SLOTS = 40


def make_tables():
    d = np.arange(128)
    ang = -2.0 * np.pi * ((d[:, None] * d[None, :]) % 128) / 128
    fr, fi = np.cos(ang), np.sin(ang)
    u = np.block([[fr, -fi], [fi, fr]])
    tables = np.stack([u, u.T]).astype(ml_dtypes.bfloat16)
    ang = -2.0 * np.pi * (d[:, None] * d[None, :]) / 16384
    t0 = np.stack([np.cos(ang), np.sin(ang)]).astype(np.float32)
    place = np.arange(16384).reshape(128, 128)
    ang = -2.0 * np.pi * (np.arange(ROWS)[:, None, None] * place[None]) / 1048576
    w1 = np.stack([np.cos(ang), np.sin(ang)], axis=1).astype(np.float32)
    pick = np.zeros((2, 2, SLOTS, 128))
    perm = np.zeros((2, 2, 64, 2, 2, 128))
    for lo in range(2):
        for k1 in range(ROWS):
            alone = k1 in (0, 32)
            pick[0, lo, k1, lo * 64 + k1] = 2.0 ** -20 if alone else 2.0 ** -21
            if not alone:
                pick[1, lo, k1, lo * 64 + 64 - k1] = 2.0 ** -21
        for hi in range(64):
            k2 = 2 * hi + lo
            for part in range(2):
                perm[0, lo, hi, part, part, k2] = 1.0
                perm[1, lo, hi, part, part, 127 - k2] = 1.0 - 2.0 * part
    pick = pick.reshape(4 * SLOTS, 128).astype(ml_dtypes.bfloat16)
    perm = perm.reshape(512, 256).astype(ml_dtypes.bfloat16)
    return tables, t0, w1, pick, perm


def times(a, b, conj=False):
    if conj:
        return (a[0] * b[0] + a[1] * b[1], a[1] * b[0] - a[0] * b[1])
    return (a[0] * b[0] - a[1] * b[1], a[0] * b[1] + a[1] * b[0])


def turn(z, k, n, orient):
    re, im = z
    if k == 0:
        return z
    if 4 * k == n:
        if im is None:
            return (None, re if orient > 0 else -re)
        return (-im, re) if orient > 0 else (im, -re)
    c = math.cos(2.0 * math.pi * k / n)
    s = orient * math.sin(2.0 * math.pi * k / n)
    if im is None:
        return (re * c, re * s)
    if 8 * k == n:
        if orient > 0:
            return ((re - im) * c, (re + im) * c)
        return ((re + im) * c, (im - re) * c)
    return (re * c - im * s, re * s + im * c)


def plus(a, b):
    if a is None:
        return b
    if b is None:
        return a
    return a + b


def minus(a, b):
    if b is None:
        return a
    if a is None:
        return -b
    return a - b


def real_forward(vals, n):
    if n == 2:
        return [(vals[0], None), (vals[0], None)]
    even = real_forward(vals[0::2], n // 2)
    odd = real_forward(vals[1::2], n // 2)
    out = [None] * (n // 2 + 1)
    for k in range(n // 4 + 1):
        t = turn(odd[k], k, n, -1)
        e = even[k]
        out[k] = (plus(e[0], t[0]), plus(e[1], t[1]))
        if n // 2 - k != k:
            out[n // 2 - k] = (minus(e[0], t[0]), minus(t[1], e[1]))
    return out


def real_inverse(bins, n):
    if n == 2:
        return [bins[0][0] + bins[1][0]]
    even, odd = [], []
    for k in range(n // 4 + 1):
        a, b = bins[k], bins[n // 2 - k]
        even.append((plus(a[0], b[0]), minus(a[1], b[1])))
        t = (minus(a[0], b[0]), plus(a[1], b[1]))
        if k == n // 4:
            even[-1] = (a[0] + a[0], None)
            t = (None, a[1] + a[1])
            odd.append(turn_imag(t[1]))
        else:
            odd.append(turn(t, k, n, 1))
    first = real_inverse(even, n // 2)
    second = real_inverse(odd, n // 2)
    out = [None] * (n // 2)
    out[0::2] = first
    out[1::2] = second
    return out


def turn_imag(im):
    return (-im, None)


def filter_step(pairs_at, h_at, sh, pick, perm, direct):
    pieces = []
    for a, b in pairs_at:
        got = {}
        for name, k3 in (("a", a), ("b", b)):
            got[name] = lax.dot_general(
                pick, h_at(k3), (((1,), (1,)), ((), ())), preferred_element_type=F32
            ).astype(BF16)
        for mine, other in (("a", "b"), ("b", "a")):
            own, mirror = got[mine], got[other]
            pieces.append(
                jnp.concatenate(
                    [
                        own[0:SLOTS],
                        own[SLOTS : 2 * SLOTS],
                        mirror[2 * SLOTS : 3 * SLOTS],
                        mirror[3 * SLOTS : 4 * SLOTS],
                    ],
                    axis=1,
                )
            )
    joined = jnp.concatenate(pieces, axis=0)
    z = jnp.dot(joined, perm, preferred_element_type=F32)
    i = 0
    for a, b in pairs_at:
        for k3 in (a, b):
            zz = z[i * SLOTS : (i + 1) * SLOTS]
            sh[pl.ds(k3, SLOTS, stride=256), :] = zz[:, :128] + direct
            sh[pl.ds(128 + k3, SLOTS, stride=256), :] = zz[:, 128:]
            i += 1


def filter_prep(h_ref, sh, hs, pick_ref, perm_ref, direct, unroll=8):
    pick = pick_ref[...]
    perm = perm_ref[...]

    def h_at(k3):
        return h_ref[pl.ds(pl.multiple_of(k3 * 128, 128), 128), :]

    def step(i, c):
        filter_step(
            [(i * unroll + j, 127 - (i * unroll + j)) for j in range(unroll)],
            h_at, sh, pick, perm, direct,
        )
        return c

    lax.fori_loop(0, 64 // unroll, step, 0)

    same = (
        lax.broadcasted_iota(jnp.int32, (128, 128), 0)
        == lax.broadcasted_iota(jnp.int32, (128, 128), 1)
    ).astype(BF16)

    def turn_over(i, c):
        planes = []
        for j in range(11):
            row = pl.multiple_of((i * 11 + j) * 256, 256)
            planes.append(sh[pl.ds(row, 256), :].astype(BF16))
        turned = [
            lax.dot_general(same, x, (((1,), (1,)), ((), ())), preferred_element_type=F32)
            for x in planes
        ]
        for j in range(11):
            for part in range(2):
                hs[i * 11 + j, part] = turned[j][:, part * 128 : (part + 1) * 128]
        return c

    lax.fori_loop(0, ROWS // 11, turn_over, 0)


def stage_one(load, a_ref, w1_ref, row, height=16):
    bins = real_forward([load(s) for s in range(32)], 64)
    for k1 in range(ROWS):
        re, im = bins[k1]
        if k1 == 0:
            im = jnp.zeros_like(re)
        else:
            wr = w1_ref[k1, 0, pl.ds(row, height), :]
            wi = w1_ref[k1, 1, pl.ds(row, height), :]
            if im is None:
                re, im = re * wr, re * wi
            else:
                re, im = times((re, im), (wr, wi))
        a_ref[k1, pl.ds(row, height), :] = re.astype(BF16)
        a_ref[k1, pl.ds(128 + row, height), :] = im.astype(BF16)


def middle(groups, a_ref, g_ref, hs, u, v, t0_ref):
    tr, ti = t0_ref[0], t0_ref[1]

    def along_lanes(re, im):
        return jnp.concatenate([re.astype(BF16), im.astype(BF16)], axis=1)

    b = [
        jnp.dot(
            u, jnp.concatenate([a_ref[k] for k in rows], axis=1), preferred_element_type=F32
        )
        for rows in groups
    ]
    lines = []
    for rows, x in zip(groups, b):
        lines.append(
            jnp.concatenate(
                [
                    along_lanes(
                        *times(
                            (x[:128, i * 128 : (i + 1) * 128], x[128:, i * 128 : (i + 1) * 128]),
                            (tr, ti),
                        )
                    )
                    for i in range(len(rows))
                ],
                axis=0,
            )
        )
    c = [jnp.dot(x, v, preferred_element_type=F32) for x in lines]
    lines = []
    for rows, x in zip(groups, c):
        lines.append(
            jnp.concatenate(
                [
                    along_lanes(
                        *times(
                            (x[i * 128 : (i + 1) * 128, :128], x[i * 128 : (i + 1) * 128, 128:]),
                            (hs[k, 0], hs[k, 1]),
                        )
                    )
                    for i, k in enumerate(rows)
                ],
                axis=0,
            )
        )
    e = [jnp.dot(x, u, preferred_element_type=F32) for x in lines]
    lines = []
    for rows, x in zip(groups, e):
        cols = []
        for i in range(len(rows)):
            re, im = times(
                (x[i * 128 : (i + 1) * 128, :128], x[i * 128 : (i + 1) * 128, 128:]),
                (tr, ti),
                conj=True,
            )
            cols.append(jnp.concatenate([re.astype(BF16), im.astype(BF16)], axis=0))
        lines.append(jnp.concatenate(cols, axis=1))
    g = [jnp.dot(v, x, preferred_element_type=F32) for x in lines]
    for rows, x in zip(groups, g):
        for i, k in enumerate(rows):
            g_ref[k] = x[:, i * 128 : (i + 1) * 128]


def all_middle(a_ref, g_ref, hs, uv_ref, t0_ref):
    u, v = uv_ref[0], uv_ref[1]
    pairs = [[2 * i, 2 * i + 1] for i in range(16)]
    middle(pairs[:8], a_ref, g_ref, hs, u, v, t0_ref)
    middle(pairs[8:] + [[32]], a_ref, g_ref, hs, u, v, t0_ref)


def stage_last(g_ref, w1_ref, row, height=16):
    bins = []
    for k1 in range(ROWS):
        re = g_ref[k1, pl.ds(row, height), :]
        im = g_ref[k1, pl.ds(128 + row, height), :]
        if k1 == 0:
            bins.append((re, None))
            continue
        wr = w1_ref[k1, 0, pl.ds(row, height), :]
        wi = w1_ref[k1, 1, pl.ds(row, height), :]
        if k1 == 32:
            bins.append((re * wr + im * wi, None))
        else:
            bins.append(times((re, im), (wr, wi), conj=True))
    return real_inverse(bins, 64)


SEQ = 32
CHAN = 8
SLAB = 16384
TILES = 4
MESH = pl.DeviceIdType.MESH
THERE = [(0, 112, 16), (1, 80, 32), (2, 48, 32), (3, 16, 32), (4, 0, 16)]
BACK = [(0, 0, 16), (1, 16, 32), (2, 48, 32), (3, 80, 32), (4, 112, 16)]
EARLY = 2


def each_peer(fn, count, per):
    def step(i, c):
        for k in range(per):
            fn(i * per + k + 1)
        return c

    whole = (count - 1) // per
    lax.fori_loop(0, whole, step, 0)
    for i in range(whole * per + 1, count):
        fn(i)


def fused(
    streams, wts, skip, h2, residual, uv_in, t0_in, w1_in, pick_in, perm_in,
    out_h, out_r,
    st, flat, sb, xb, hv, sh, hs, a, g, uv, t0, w1, pick, perm, yb, rb,
    gate, res, hb, sqp, sqa, rs, wb,
    piece_sem, load_sem, halo_sem, x_send, x_recv, y_send, y_recv, s_send, s_recv, o_sem,
):
    me = lax.axis_index("seq")
    mc = lax.axis_index("chan")

    def seq_peer(i):
        return lax.rem(me + i * 11, SEQ)

    def chan_peer(i):
        return lax.rem(mc + i, CHAN)

    def stream_piece(n, first, tiles):
        here = pl.ds(first * 128, tiles * 128)
        there = pl.ds(first * 128 + 128, tiles * 128)
        return pltpu.make_async_copy(
            streams.at[pl.ds(1, 2), :, here], st.at[pl.ds(1, 2), :, there], piece_sem.at[n]
        )

    pieces = [
        stream_piece(0, 111, 17),
        stream_piece(1, 79, 32),
        stream_piece(2, 47, 32),
        stream_piece(3, 15, 32),
        stream_piece(4, 0, 15),
    ]
    loads = [
        pltpu.make_async_copy(h2, hv, load_sem.at[0]),
        pltpu.make_async_copy(pick_in, pick, load_sem.at[1]),
        pltpu.make_async_copy(perm_in, perm, load_sem.at[2]),
        pltpu.make_async_copy(
            streams.at[pl.ds(0, 1)], st.at[pl.ds(0, 1), :, pl.ds(128, SLAB)], load_sem.at[3]
        ),
        pltpu.make_async_copy(w1_in, w1, load_sem.at[4]),
        pltpu.make_async_copy(uv_in, uv, load_sem.at[5]),
        pltpu.make_async_copy(t0_in, t0, load_sem.at[6]),
        pltpu.make_async_copy(residual, res, load_sem.at[7]),
    ]
    for copy in pieces:
        copy.start()

    barrier = pltpu.get_barrier_semaphore()

    def greet_seq(i):
        pl.semaphore_signal(
            barrier, inc=1, device_id={"seq": lax.rem(me + i, SEQ)}, device_id_type=MESH
        )

    def greet_chan(i):
        pl.semaphore_signal(barrier, inc=1, device_id={"chan": chan_peer(i)}, device_id_type=MESH)

    each_peer(greet_seq, SEQ, 5)
    each_peer(greet_chan, CHAN, 7)

    eye = lax.broadcasted_iota(jnp.int32, (32, 32), 0) == lax.broadcasted_iota(
        jnp.int32, (32, 32), 1
    )

    def spread(row):
        column = jnp.sum(jnp.where(eye, row, 0.0), axis=1, keepdims=True)
        return jnp.broadcast_to(column, (32, 128))

    for stream in range(3):
        for tap in range(3):
            wb[stream * 3 + tap] = spread(wts[stream, pl.ds(tap, 1), :])

    lane = lax.broadcasted_iota(jnp.int32, (32, 128), 1)

    def short_conv(stream, first):
        cur = [
            st[stream, :, pl.ds(pl.multiple_of((first + i) * 128, 128), 128)].astype(F32)
            for i in range(TILES + 1)
        ]
        one = [pltpu.roll(t, 1, 1) for t in cur]
        two = [pltpu.roll(t, 2, 1) for t in cur]
        out = []
        for i in range(1, TILES + 1):
            back1 = jnp.where(lane < 1, one[i - 1], one[i])
            back2 = jnp.where(lane < 2, two[i - 1], two[i])
            out.append(
                wb[stream * 3] * cur[i] + wb[stream * 3 + 1] * back1 + wb[stream * 3 + 2] * back2
            )
        return out

    def gate_rows(start, rows):
        def gate_in(i, c):
            first = start + i * TILES
            one, two = short_conv(1, first), short_conv(2, first)
            for k in range(TILES):
                flat[pl.ds(pl.multiple_of((first + k) * 32, 32), 32), :] = one[k] * two[k]
            return c

        lax.fori_loop(0, rows // TILES, gate_in, 0)

    def one_row(start, rows, c):
        return flat[pl.ds(start * 32 + c, rows, stride=32), :].astype(BF16)

    def prepare(start, rows):
        span = pl.ds(pl.multiple_of(start, 16), rows)

        def take(c):
            sb[c, span, :] = one_row(start, rows, c)

        def step(i, c):
            for k in range(4):
                take(i * 4 + k)
            return c

        lax.fori_loop(0, 8, step, 0)
        xb[me, span, :] = sb[me, span, :]

    def send_to(peer, n, start, rows):
        span = pl.ds(pl.multiple_of(start, 16), rows)
        pltpu.make_async_remote_copy(
            src_ref=sb.at[peer, span],
            dst_ref=xb.at[me, span],
            send_sem=x_send.at[n],
            recv_sem=x_recv.at[n],
            device_id={"seq": peer},
            device_id_type=MESH,
        ).start()

    def send_rows(core, n, start, rows):
        def send(i):
            send_to(lax.rem(me // 2 + i * 5, SEQ // 2) * 2 + core, n, start, rows)

        each_peer(send, SEQ // 2, 5)

    def first_sends(n, start, rows):
        prepare(start, rows)
        send_rows(0, n, start, rows)
        send_to(me + 1 - 2 * lax.rem(me, 2), n, start, rows)

    pieces[0].wait()
    gate_rows(112, 16)
    pl.semaphore_wait(barrier, SEQ + CHAN - 2)
    halo = pltpu.make_async_remote_copy(
        src_ref=streams.at[:, :, pl.ds(SLAB - 128, 128)],
        dst_ref=st.at[:, :, pl.ds(0, 128)],
        send_sem=halo_sem.at[0],
        recv_sem=halo_sem.at[1],
        device_id={"seq": lax.rem(me + 1, SEQ)},
        device_id_type=MESH,
    )
    halo.start()
    first_sends(0, 112, 16)
    for i in range(1, 5):
        pieces[i].wait()
    for copy in loads:
        copy.start()

    def send_more(n, c):
        start = 112 - n * 32
        gate_rows(start, 32)
        first_sends(n, start, 32)
        return c

    lax.fori_loop(1, 4, send_more, 0)
    halo.wait()
    rim = st[:, :, pl.ds(0, 128)]
    st[:, :, pl.ds(0, 128)] = jnp.where(me > 0, rim, jnp.zeros_like(rim))
    gate_rows(0, 16)
    first_sends(4, 0, 16)

    def second_sends(n, c):
        send_rows(1, n, 112 - n * 32, 32)
        return c

    send_rows(1, 0, 112, 16)
    lax.fori_loop(1, 4, second_sends, 0)
    send_rows(1, 4, 0, 16)

    for i in (0, 1, 2):
        loads[i].wait()
    filter_prep(hv, sh, hs, pick, perm, skip[me] * 2.0**-20)
    for i in (4, 5, 6):
        loads[i].wait()

    def all_of(buf, start, rows, sem):
        part = buf.at[pl.ds(0, SEQ - 1), pl.ds(pl.multiple_of(start, 16), rows)]
        return pltpu.make_async_copy(part, part, sem)

    def transform_rows(n, start, rows):
        all_of(xb, start, rows, x_recv.at[n]).wait()

        def part(k, c):
            r = pl.multiple_of(start + k * 16, 16)
            stage_one(lambda s: xb[s, pl.ds(r, 16), :].astype(F32), a, w1, r)
            return c

        lax.fori_loop(0, rows // 16, part, 0)

    def transform_more(n, c):
        transform_rows(n, 112 - n * 32, 32)
        return c

    transform_rows(0, 112, 16)
    lax.fori_loop(1, 4, transform_more, 0)
    transform_rows(4, 0, 16)
    all_middle(a, g, hs, uv, t0)

    def back_rows(start, rows):
        def part(k, c):
            r = pl.multiple_of(start + k * 16, 16)
            ys = stage_last(g, w1, r)
            for s in range(SEQ):
                yb[s, pl.ds(r, 16), :] = ys[s].astype(BF16)
            return c

        lax.fori_loop(0, rows // 16, part, 0)
        span = pl.ds(pl.multiple_of(start, 16), rows)
        rb[me, span, :] = yb[me, span, :]

    def send_back(peer, n, start, rows):
        span = pl.ds(pl.multiple_of(start, 16), rows)
        pltpu.make_async_remote_copy(
            src_ref=yb.at[peer, span],
            dst_ref=rb.at[me, span],
            send_sem=y_send.at[n],
            recv_sem=y_recv.at[n],
            device_id={"seq": peer},
            device_id_type=MESH,
        ).start()

    def back_more(n, c):
        start = n * 32 - 16
        back_rows(start, 32)
        each_peer(lambda i: send_back(seq_peer(i), n, start, 32), SEQ, 5)
        return c

    def z_of(peer):
        return lax.rem(peer // 2, 8)

    def to_early(i):
        peer = seq_peer(i)

        @pl.when(z_of(peer) < EARLY)
        def _():
            send_back(peer, *BACK[3])
            send_back(peer, *BACK[4])

    def to_late(chunk):
        def send(i):
            peer = seq_peer(i)

            @pl.when(z_of(peer) >= EARLY)
            def _():
                send_back(peer, *chunk)

        return send

    back_rows(0, 16)
    each_peer(lambda i: send_back(seq_peer(i), *BACK[0]), SEQ, 5)
    lax.fori_loop(1, 3, back_more, 0)
    back_rows(80, 48)
    each_peer(to_early, SEQ, 5)
    each_peer(to_late(BACK[3]), SEQ, 5)
    each_peer(to_late(BACK[4]), SEQ, 5)

    for i in (3, 7):
        loads[i].wait()

    def gate_tiles(i, c):
        first = i * TILES
        vals = short_conv(0, first)
        for k in range(TILES):
            gate[:, pl.ds(pl.multiple_of((first + k) * 128, 128), 128)] = vals[k].astype(BF16)
        return c

    lax.fori_loop(0, 128 // TILES, gate_tiles, 0)
    def sums_of(start, rows, sem):
        part = sqa.at[pl.ds(0, CHAN - 1), pl.ds(pl.multiple_of(start, 16), rows)]
        return pltpu.make_async_copy(part, part, sem)

    def hidden_out(n, start, rows):
        cols = pl.ds(pl.multiple_of(start * 128, 128), rows * 128)
        return pltpu.make_async_copy(hb.at[:, cols], out_h.at[:, cols], o_sem.at[n])

    def combine(n, start, rows):
        all_of(rb, start, rows, y_recv.at[n]).wait()
        span = pl.ds(pl.multiple_of(start, 16), rows)

        def spread_row(ch, c):
            flat[pl.ds(start * 32 + ch, rows, stride=32), :] = rb[ch, span, :].astype(F32)
            return c

        lax.fori_loop(0, 32, spread_row, 0, unroll=8)

        def tile(r, c):
            p = start + r
            cols = pl.ds(pl.multiple_of(p * 128, 128), 128)
            long_out = flat[pl.ds(pl.multiple_of(p * 32, 32), 32), :]
            hidden = (res[:, cols].astype(F32) + gate[:, cols].astype(F32) * long_out).astype(BF16)
            hb[:, cols] = hidden
            wide = hidden.astype(F32)
            sqp[pl.ds(p, 1), :] = jnp.sum(wide * wide, axis=0, keepdims=True)
            return c

        lax.fori_loop(0, rows, tile, 0, unroll=8)

        def send(i):
            pltpu.make_async_remote_copy(
                src_ref=sqp.at[span],
                dst_ref=sqa.at[mc, span],
                send_sem=s_send.at[n],
                recv_sem=s_recv.at[n],
                device_id={"chan": chan_peer(i)},
                device_id_type=MESH,
            ).start()

        each_peer(send, CHAN, 7)
        sqa[mc, span, :] = sqp[span, :]
        hidden_out(n, start, rows).start()

    def norm(n, start, rows):
        sums_of(start, rows, s_recv.at[n]).wait()
        span = pl.ds(pl.multiple_of(start, 16), rows)
        total = sqa[0, span, :]
        for k in range(1, CHAN):
            total = total + sqa[k, span, :]
        rs[span, :] = lax.rsqrt(total * (1.0 / (32 * CHAN)) + 1e-06)

    def combine_more(n, c):
        combine(n, n * 32 - 16, 32)
        return c

    def norm_more(n, c):
        norm(n, n * 32 - 16, 32)
        return c

    combine(0, 0, 16)
    lax.fori_loop(1, 4, combine_more, 0)
    combine(4, 112, 16)
    norm(0, 0, 16)
    lax.fori_loop(1, 4, norm_more, 0)
    norm(4, 112, 16)
    scale_out = pltpu.make_async_copy(rs, out_r, o_sem.at[5])
    scale_out.start()
    for n, start, rows in THERE:
        all_of(xb, start, rows, x_send.at[n]).wait()
    for n, start, rows in BACK:
        all_of(rb, start, rows, y_send.at[n]).wait()
        sums_of(start, rows, s_send.at[n]).wait()
        hidden_out(n, start, rows).wait()
    scale_out.wait()


PARTS = 4


def finish(hidden, scale, gain, out_h, out_n, hb, nb, rs, gb, in_sem, out_sem):
    size = SLAB // PARTS

    def cols(j):
        return pl.ds(j * size, size)

    scale_in = pltpu.make_async_copy(scale, rs, in_sem.at[PARTS])
    scale_in.start()
    ins = [
        pltpu.make_async_copy(hidden.at[:, cols(j)], hb.at[:, cols(j)], in_sem.at[j])
        for j in range(PARTS)
    ]
    for copy in ins:
        copy.start()
    eye = lax.broadcasted_iota(jnp.int32, (32, 32), 0) == lax.broadcasted_iota(
        jnp.int32, (32, 32), 1
    )
    column = jnp.sum(jnp.where(eye, gain[...], 0.0), axis=1, keepdims=True)
    gb[...] = jnp.broadcast_to(column, (32, 128))
    scale_in.wait()
    outs = []
    for j in range(PARTS):
        ins[j].wait()
        outs.append(pltpu.make_async_copy(hb.at[:, cols(j)], out_h.at[:, cols(j)], out_sem.at[0, j]))
        outs[-1].start()

        def tile(r, c):
            p = j * (128 // PARTS) + r
            here = pl.ds(pl.multiple_of(p * 128, 128), 128)
            nb[:, here] = (hb[:, here].astype(F32) * (gb[...] * rs[pl.ds(p, 1), :])).astype(BF16)
            return c

        lax.fori_loop(0, 128 // PARTS, tile, 0, unroll=8)
        outs.append(pltpu.make_async_copy(nb.at[:, cols(j)], out_n.at[:, cols(j)], out_sem.at[1, j]))
        outs[-1].start()
    for copy in outs:
        copy.wait()


def per_device(streams, conv_weights, skip, filter_spec, residual, gain):
    tables = [jnp.asarray(t) for t in make_tables()]
    h2 = filter_spec.reshape(2, 8192, 128).transpose(1, 0, 2).reshape(16384, 128)
    far = pl.BlockSpec(memory_space=pl.ANY)
    near = pl.BlockSpec(memory_space=pltpu.VMEM)
    slab = (32, SLAB)
    dma = pltpu.SemaphoreType.DMA
    vmem = pltpu.VMEM
    line = gain.reshape(1, 32)
    hidden, scale = pl.pallas_call(
        fused,
        out_shape=[
            jax.ShapeDtypeStruct(slab, BF16),
            jax.ShapeDtypeStruct((128, 128), F32),
        ],
        in_specs=[far, near, pl.BlockSpec(memory_space=pltpu.SMEM)] + [far] * 7,
        out_specs=[far, far],
        scratch_shapes=[
            vmem((3, 32, 128 + SLAB), BF16),
            vmem((4096, 128), F32),
            vmem((32, 128, 128), BF16),
            vmem((32, 128, 128), BF16),
            vmem((16384, 128), BF16),
            vmem((SLOTS * 256, 128), F32),
            vmem((ROWS, 2, 128, 128), F32),
            vmem((ROWS, 256, 128), BF16),
            vmem((ROWS, 256, 128), F32),
            vmem((2, 256, 256), BF16),
            vmem((2, 128, 128), F32),
            vmem((ROWS, 2, 128, 128), F32),
            vmem((4 * SLOTS, 128), BF16),
            vmem((512, 256), BF16),
            vmem((32, 128, 128), BF16),
            vmem((32, 128, 128), BF16),
            vmem(slab, BF16),
            vmem(slab, BF16),
            vmem(slab, BF16),
            vmem((128, 128), F32),
            vmem((CHAN, 128, 128), F32),
            vmem((128, 128), F32),
            vmem((9, 32, 128), F32),
            dma((5,)),
            dma((8,)),
            dma((2,)),
            dma((5,)),
            dma((5,)),
            dma((5,)),
            dma((5,)),
            dma((5,)),
            dma((5,)),
            dma((6,)),
        ],
        compiler_params=pltpu.CompilerParams(
            collective_id=0, has_side_effects=True, vmem_limit_bytes=60 * 2**20
        ),
        cost_estimate=pl.CostEstimate(
            flops=8 * 10**9, bytes_accessed=20 * 2**20, transcendentals=0
        ),
    )(streams, conv_weights.transpose(0, 2, 1), skip, h2, residual, *tables)
    return pl.pallas_call(
        finish,
        out_shape=[jax.ShapeDtypeStruct(slab, BF16)] * 2,
        in_specs=[far, far, near],
        out_specs=[far, far],
        scratch_shapes=[
            vmem(slab, BF16),
            vmem(slab, BF16),
            vmem((128, 128), F32),
            vmem((32, 128), F32),
            dma((PARTS + 1,)),
            dma((2, PARTS)),
        ],
        compiler_params=pltpu.CompilerParams(vmem_limit_bytes=60 * 2**20),
        cost_estimate=pl.CostEstimate(
            flops=3 * 2**19, bytes_accessed=3 * 2**20, transcendentals=0
        ),
    )(hidden, scale, line)


def solution(mesh):
    in_specs = (
        P(None, "chan", "seq"),
        P(None, "chan", None),
        P("chan"),
        P("chan", "seq", None, None),
        P("chan", "seq"),
        P("chan"),
    )
    return jax.shard_map(
        lambda *args: tuple(per_device(*args)),
        mesh=mesh,
        in_specs=in_specs,
        out_specs=(P("chan", "seq"), P("chan", "seq")),
        check_vma=False,
    )
```

```python
import math
import numpy as np
import jax
import jax.numpy as jnp
from jax import lax
from jax.experimental import pallas as pl
from jax.experimental.pallas import tpu as pltpu
import ml_dtypes
from jax.sharding import PartitionSpec as P

F32 = jnp.float32
BF16 = jnp.bfloat16
ROWS = 33
SLOTS = 40


def make_tables():
    d = np.arange(128)
    ang = -2.0 * np.pi * ((d[:, None] * d[None, :]) % 128) / 128
    fr, fi = np.cos(ang), np.sin(ang)
    u = np.block([[fr, -fi], [fi, fr]])
    tables = np.stack([u, u.T]).astype(ml_dtypes.bfloat16)
    ang = -2.0 * np.pi * (d[:, None] * d[None, :]) / 16384
    t0 = np.stack([np.cos(ang), np.sin(ang)]).astype(np.float32)
    place = np.arange(16384).reshape(128, 128)
    ang = -2.0 * np.pi * (np.arange(ROWS)[:, None, None] * place[None]) / 1048576
    w1 = np.stack([np.cos(ang), np.sin(ang)], axis=1).astype(np.float32)
    pick = np.zeros((2, 2, SLOTS, 128))
    perm = np.zeros((2, 2, 64, 2, 2, 128))
    for lo in range(2):
        for k1 in range(ROWS):
            alone = k1 in (0, 32)
            pick[0, lo, k1, lo * 64 + k1] = 2.0 ** -20 if alone else 2.0 ** -21
            if not alone:
                pick[1, lo, k1, lo * 64 + 64 - k1] = 2.0 ** -21
        for hi in range(64):
            k2 = 2 * hi + lo
            for part in range(2):
                perm[0, lo, hi, part, part, k2] = 1.0
                perm[1, lo, hi, part, part, 127 - k2] = 1.0 - 2.0 * part
    pick = pick.reshape(4 * SLOTS, 128).astype(ml_dtypes.bfloat16)
    perm = perm.reshape(512, 256).astype(ml_dtypes.bfloat16)
    return tables, t0, w1, pick, perm


def times(a, b, conj=False):
    if conj:
        return (a[0] * b[0] + a[1] * b[1], a[1] * b[0] - a[0] * b[1])
    return (a[0] * b[0] - a[1] * b[1], a[0] * b[1] + a[1] * b[0])


def turn(z, k, n, orient):
    re, im = z
    if k == 0:
        return z
    if 4 * k == n:
        if im is None:
            return (None, re if orient > 0 else -re)
        return (-im, re) if orient > 0 else (im, -re)
    c = math.cos(2.0 * math.pi * k / n)
    s = orient * math.sin(2.0 * math.pi * k / n)
    if im is None:
        return (re * c, re * s)
    if 8 * k == n:
        if orient > 0:
            return ((re - im) * c, (re + im) * c)
        return ((re + im) * c, (im - re) * c)
    return (re * c - im * s, re * s + im * c)


def plus(a, b):
    if a is None:
        return b
    if b is None:
        return a
    return a + b


def minus(a, b):
    if b is None:
        return a
    if a is None:
        return -b
    return a - b


def real_forward(vals, n):
    if n == 2:
        return [(vals[0], None), (vals[0], None)]
    even = real_forward(vals[0::2], n // 2)
    odd = real_forward(vals[1::2], n // 2)
    out = [None] * (n // 2 + 1)
    for k in range(n // 4 + 1):
        t = turn(odd[k], k, n, -1)
        e = even[k]
        out[k] = (plus(e[0], t[0]), plus(e[1], t[1]))
        if n // 2 - k != k:
            out[n // 2 - k] = (minus(e[0], t[0]), minus(t[1], e[1]))
    return out


def real_inverse(bins, n):
    if n == 2:
        return [bins[0][0] + bins[1][0]]
    even, odd = [], []
    for k in range(n // 4 + 1):
        a, b = bins[k], bins[n // 2 - k]
        even.append((plus(a[0], b[0]), minus(a[1], b[1])))
        t = (minus(a[0], b[0]), plus(a[1], b[1]))
        if k == n // 4:
            even[-1] = (a[0] + a[0], None)
            t = (None, a[1] + a[1])
            odd.append(turn_imag(t[1]))
        else:
            odd.append(turn(t, k, n, 1))
    first = real_inverse(even, n // 2)
    second = real_inverse(odd, n // 2)
    out = [None] * (n // 2)
    out[0::2] = first
    out[1::2] = second
    return out


def turn_imag(im):
    return (-im, None)


def filter_step(pairs_at, h_at, sh, pick, perm, direct):
    pieces = []
    for a, b in pairs_at:
        got = {}
        for name, k3 in (("a", a), ("b", b)):
            got[name] = lax.dot_general(
                pick, h_at(k3), (((1,), (1,)), ((), ())), preferred_element_type=F32
            ).astype(BF16)
        for mine, other in (("a", "b"), ("b", "a")):
            own, mirror = got[mine], got[other]
            pieces.append(
                jnp.concatenate(
                    [
                        own[0:SLOTS],
                        own[SLOTS : 2 * SLOTS],
                        mirror[2 * SLOTS : 3 * SLOTS],
                        mirror[3 * SLOTS : 4 * SLOTS],
                    ],
                    axis=1,
                )
            )
    joined = jnp.concatenate(pieces, axis=0)
    z = jnp.dot(joined, perm, preferred_element_type=F32)
    i = 0
    for a, b in pairs_at:
        for k3 in (a, b):
            zz = z[i * SLOTS : (i + 1) * SLOTS]
            sh[pl.ds(k3, SLOTS, stride=256), :] = zz[:, :128] + direct
            sh[pl.ds(128 + k3, SLOTS, stride=256), :] = zz[:, 128:]
            i += 1


def filter_prep(h_ref, sh, hs, pick_ref, perm_ref, direct, unroll=8):
    pick = pick_ref[...]
    perm = perm_ref[...]

    def h_at(k3):
        return h_ref[pl.ds(pl.multiple_of(k3 * 128, 128), 128), :]

    def step(i, c):
        filter_step(
            [(i * unroll + j, 127 - (i * unroll + j)) for j in range(unroll)],
            h_at, sh, pick, perm, direct,
        )
        return c

    lax.fori_loop(0, 64 // unroll, step, 0)

    same = (
        lax.broadcasted_iota(jnp.int32, (128, 128), 0)
        == lax.broadcasted_iota(jnp.int32, (128, 128), 1)
    ).astype(BF16)

    def turn_over(i, c):
        planes = []
        for j in range(11):
            row = pl.multiple_of((i * 11 + j) * 256, 256)
            planes.append(sh[pl.ds(row, 256), :].astype(BF16))
        turned = [
            lax.dot_general(same, x, (((1,), (1,)), ((), ())), preferred_element_type=F32)
            for x in planes
        ]
        for j in range(11):
            for part in range(2):
                hs[i * 11 + j, part] = turned[j][:, part * 128 : (part + 1) * 128]
        return c

    lax.fori_loop(0, ROWS // 11, turn_over, 0)


def stage_one(load, a_ref, w1_ref, row, height=16):
    bins = real_forward([load(s) for s in range(32)], 64)
    for k1 in range(ROWS):
        re, im = bins[k1]
        if k1 == 0:
            im = jnp.zeros_like(re)
        else:
            wr = w1_ref[k1, 0, pl.ds(row, height), :]
            wi = w1_ref[k1, 1, pl.ds(row, height), :]
            if im is None:
                re, im = re * wr, re * wi
            else:
                re, im = times((re, im), (wr, wi))
        a_ref[k1, pl.ds(row, height), :] = re.astype(BF16)
        a_ref[k1, pl.ds(128 + row, height), :] = im.astype(BF16)


def middle(groups, a_ref, g_ref, hs, u, v, t0_ref):
    tr, ti = t0_ref[0], t0_ref[1]

    def along_lanes(re, im):
        return jnp.concatenate([re.astype(BF16), im.astype(BF16)], axis=1)

    b = [
        jnp.dot(
            u, jnp.concatenate([a_ref[k] for k in rows], axis=1), preferred_element_type=F32
        )
        for rows in groups
    ]
    lines = []
    for rows, x in zip(groups, b):
        lines.append(
            jnp.concatenate(
                [
                    along_lanes(
                        *times(
                            (x[:128, i * 128 : (i + 1) * 128], x[128:, i * 128 : (i + 1) * 128]),
                            (tr, ti),
                        )
                    )
                    for i in range(len(rows))
                ],
                axis=0,
            )
        )
    c = [jnp.dot(x, v, preferred_element_type=F32) for x in lines]
    lines = []
    for rows, x in zip(groups, c):
        lines.append(
            jnp.concatenate(
                [
                    along_lanes(
                        *times(
                            (x[i * 128 : (i + 1) * 128, :128], x[i * 128 : (i + 1) * 128, 128:]),
                            (hs[k, 0], hs[k, 1]),
                        )
                    )
                    for i, k in enumerate(rows)
                ],
                axis=0,
            )
        )
    e = [jnp.dot(x, u, preferred_element_type=F32) for x in lines]
    lines = []
    for rows, x in zip(groups, e):
        cols = []
        for i in range(len(rows)):
            re, im = times(
                (x[i * 128 : (i + 1) * 128, :128], x[i * 128 : (i + 1) * 128, 128:]),
                (tr, ti),
                conj=True,
            )
            cols.append(jnp.concatenate([re.astype(BF16), im.astype(BF16)], axis=0))
        lines.append(jnp.concatenate(cols, axis=1))
    g = [jnp.dot(v, x, preferred_element_type=F32) for x in lines]
    for rows, x in zip(groups, g):
        for i, k in enumerate(rows):
            g_ref[k] = x[:, i * 128 : (i + 1) * 128]


def all_middle(a_ref, g_ref, hs, uv_ref, t0_ref):
    u, v = uv_ref[0], uv_ref[1]
    pairs = [[2 * i, 2 * i + 1] for i in range(16)]
    middle(pairs[:8], a_ref, g_ref, hs, u, v, t0_ref)
    middle(pairs[8:] + [[32]], a_ref, g_ref, hs, u, v, t0_ref)


def stage_last(g_ref, w1_ref, row, height=16):
    bins = []
    for k1 in range(ROWS):
        re = g_ref[k1, pl.ds(row, height), :]
        im = g_ref[k1, pl.ds(128 + row, height), :]
        if k1 == 0:
            bins.append((re, None))
            continue
        wr = w1_ref[k1, 0, pl.ds(row, height), :]
        wi = w1_ref[k1, 1, pl.ds(row, height), :]
        if k1 == 32:
            bins.append((re * wr + im * wi, None))
        else:
            bins.append(times((re, im), (wr, wi), conj=True))
    return real_inverse(bins, 64)


SEQ = 32
CHAN = 8
SLAB = 16384
TILES = 4
MESH = pl.DeviceIdType.MESH
THERE = [(0, 112, 16), (1, 80, 32), (2, 48, 32), (3, 16, 32), (4, 0, 16)]
BACK = [(0, 0, 16), (1, 16, 32), (2, 48, 32), (3, 80, 32), (4, 112, 16)]
LAST = [(0, 1, 3), (0, 1, 4), (1, 3, 3), (1, 3, 4), (3, 8, 3), (3, 8, 4)]


def each_peer(fn, count, per):
    def step(i, c):
        for k in range(per):
            fn(i * per + k + 1)
        return c

    whole = (count - 1) // per
    lax.fori_loop(0, whole, step, 0)
    for i in range(whole * per + 1, count):
        fn(i)


def fused(
    streams, wts, skip, h2, residual, gain, uv_in, t0_in, w1_in, pick_in, perm_in,
    hb, nb,
    st, flat, sb, xb, hv, sh, hs, a, g, uv, t0, w1, pick, perm, yb, rb,
    gate, res, sqp, sqa, rs, wb,
    piece_sem, load_sem, halo_sem, x_send, x_recv, y_send, y_recv, s_send, s_recv,
):
    me = lax.axis_index("seq")
    mc = lax.axis_index("chan")

    def seq_peer(i):
        return lax.rem(me + i * 11, SEQ)

    def chan_peer(i):
        return lax.rem(mc + i, CHAN)

    def stream_piece(n, first, tiles):
        here = pl.ds(first * 128, tiles * 128)
        there = pl.ds(first * 128 + 128, tiles * 128)
        return pltpu.make_async_copy(
            streams.at[pl.ds(1, 2), :, here], st.at[pl.ds(1, 2), :, there], piece_sem.at[n]
        )

    pieces = [
        stream_piece(0, 111, 17),
        stream_piece(1, 79, 32),
        stream_piece(2, 47, 32),
        stream_piece(3, 15, 32),
        stream_piece(4, 0, 15),
    ]
    loads = [
        pltpu.make_async_copy(h2, hv, load_sem.at[0]),
        pltpu.make_async_copy(pick_in, pick, load_sem.at[1]),
        pltpu.make_async_copy(perm_in, perm, load_sem.at[2]),
        pltpu.make_async_copy(
            streams.at[pl.ds(0, 1)], st.at[pl.ds(0, 1), :, pl.ds(128, SLAB)], load_sem.at[3]
        ),
        pltpu.make_async_copy(w1_in, w1, load_sem.at[4]),
        pltpu.make_async_copy(uv_in, uv, load_sem.at[5]),
        pltpu.make_async_copy(t0_in, t0, load_sem.at[6]),
        pltpu.make_async_copy(residual, res, load_sem.at[7]),
    ]
    for copy in pieces:
        copy.start()

    barrier = pltpu.get_barrier_semaphore()

    def greet_seq(i):
        pl.semaphore_signal(
            barrier, inc=1, device_id={"seq": lax.rem(me + i, SEQ)}, device_id_type=MESH
        )

    def greet_chan(i):
        pl.semaphore_signal(barrier, inc=1, device_id={"chan": chan_peer(i)}, device_id_type=MESH)

    each_peer(greet_seq, SEQ, 5)
    each_peer(greet_chan, CHAN, 7)

    eye = lax.broadcasted_iota(jnp.int32, (32, 32), 0) == lax.broadcasted_iota(
        jnp.int32, (32, 32), 1
    )

    def spread(row):
        column = jnp.sum(jnp.where(eye, row, 0.0), axis=1, keepdims=True)
        return jnp.broadcast_to(column, (32, 128))

    for stream in range(3):
        for tap in range(3):
            wb[stream * 3 + tap] = spread(wts[stream, pl.ds(tap, 1), :])
    wb[9] = spread(gain[...])

    lane = lax.broadcasted_iota(jnp.int32, (32, 128), 1)

    def short_conv(stream, first):
        cur = [
            st[stream, :, pl.ds(pl.multiple_of((first + i) * 128, 128), 128)].astype(F32)
            for i in range(TILES + 1)
        ]
        one = [pltpu.roll(t, 1, 1) for t in cur]
        two = [pltpu.roll(t, 2, 1) for t in cur]
        out = []
        for i in range(1, TILES + 1):
            back1 = jnp.where(lane < 1, one[i - 1], one[i])
            back2 = jnp.where(lane < 2, two[i - 1], two[i])
            out.append(
                wb[stream * 3] * cur[i] + wb[stream * 3 + 1] * back1 + wb[stream * 3 + 2] * back2
            )
        return out

    def gate_rows(start, rows):
        def gate_in(i, c):
            first = start + i * TILES
            one, two = short_conv(1, first), short_conv(2, first)
            for k in range(TILES):
                flat[pl.ds(pl.multiple_of((first + k) * 32, 32), 32), :] = one[k] * two[k]
            return c

        lax.fori_loop(0, rows // TILES, gate_in, 0)

    def one_row(start, rows, c):
        return flat[pl.ds(start * 32 + c, rows, stride=32), :].astype(BF16)

    def prepare(start, rows):
        span = pl.ds(pl.multiple_of(start, 16), rows)

        def take(c):
            sb[c, span, :] = one_row(start, rows, c)

        def step(i, c):
            for k in range(4):
                take(i * 4 + k)
            return c

        lax.fori_loop(0, 8, step, 0)
        xb[me, span, :] = sb[me, span, :]

    def send_to(peer, n, start, rows):
        span = pl.ds(pl.multiple_of(start, 16), rows)
        pltpu.make_async_remote_copy(
            src_ref=sb.at[peer, span],
            dst_ref=xb.at[me, span],
            send_sem=x_send.at[n],
            recv_sem=x_recv.at[n],
            device_id={"seq": peer},
            device_id_type=MESH,
        ).start()

    def send_rows(core, n, start, rows):
        def send(i):
            send_to(lax.rem(me // 2 + i * 5, SEQ // 2) * 2 + core, n, start, rows)

        each_peer(send, SEQ // 2, 5)

    def first_sends(n, start, rows):
        prepare(start, rows)
        send_rows(0, n, start, rows)
        send_to(me + 1 - 2 * lax.rem(me, 2), n, start, rows)

    pieces[0].wait()
    gate_rows(112, 16)
    pl.semaphore_wait(barrier, SEQ + CHAN - 2)
    halo = pltpu.make_async_remote_copy(
        src_ref=streams.at[:, :, pl.ds(SLAB - 128, 128)],
        dst_ref=st.at[:, :, pl.ds(0, 128)],
        send_sem=halo_sem.at[0],
        recv_sem=halo_sem.at[1],
        device_id={"seq": lax.rem(me + 1, SEQ)},
        device_id_type=MESH,
    )
    halo.start()
    first_sends(0, 112, 16)
    for i in range(1, 5):
        pieces[i].wait()
    for copy in loads:
        copy.start()

    def send_more(n, c):
        start = 112 - n * 32
        gate_rows(start, 32)
        first_sends(n, start, 32)
        return c

    lax.fori_loop(1, 4, send_more, 0)
    halo.wait()
    rim = st[:, :, pl.ds(0, 128)]
    st[:, :, pl.ds(0, 128)] = jnp.where(me > 0, rim, jnp.zeros_like(rim))
    gate_rows(0, 16)
    first_sends(4, 0, 16)

    def second_sends(n, c):
        send_rows(1, n, 112 - n * 32, 32)
        return c

    send_rows(1, 0, 112, 16)
    lax.fori_loop(1, 4, second_sends, 0)
    send_rows(1, 4, 0, 16)

    for i in (0, 1, 2):
        loads[i].wait()
    filter_prep(hv, sh, hs, pick, perm, skip[me] * 2.0**-20)
    for i in (4, 5, 6):
        loads[i].wait()

    def all_of(buf, start, rows, sem):
        part = buf.at[pl.ds(0, SEQ - 1), pl.ds(pl.multiple_of(start, 16), rows)]
        return pltpu.make_async_copy(part, part, sem)

    def transform_rows(n, start, rows):
        all_of(xb, start, rows, x_recv.at[n]).wait()

        def part(k, c):
            r = pl.multiple_of(start + k * 16, 16)
            stage_one(lambda s: xb[s, pl.ds(r, 16), :].astype(F32), a, w1, r)
            return c

        lax.fori_loop(0, rows // 16, part, 0)

    def transform_more(n, c):
        transform_rows(n, 112 - n * 32, 32)
        return c

    transform_rows(0, 112, 16)
    lax.fori_loop(1, 4, transform_more, 0)
    transform_rows(4, 0, 16)
    all_middle(a, g, hs, uv, t0)

    def back_rows(start, rows):
        def part(k, c):
            r = pl.multiple_of(start + k * 16, 16)
            ys = stage_last(g, w1, r)
            for s in range(SEQ):
                yb[s, pl.ds(r, 16), :] = ys[s].astype(BF16)
            return c

        lax.fori_loop(0, rows // 16, part, 0)
        span = pl.ds(pl.multiple_of(start, 16), rows)
        rb[me, span, :] = yb[me, span, :]

    def send_back(peer, n, start, rows):
        span = pl.ds(pl.multiple_of(start, 16), rows)
        pltpu.make_async_remote_copy(
            src_ref=yb.at[peer, span],
            dst_ref=rb.at[me, span],
            send_sem=y_send.at[n],
            recv_sem=y_recv.at[n],
            device_id={"seq": peer},
            device_id_type=MESH,
        ).start()

    def back_more(n, c):
        start = n * 32 - 16
        back_rows(start, 32)
        each_peer(lambda i: send_back(seq_peer(i), n, start, 32), SEQ, 5)
        return c

    def z_of(peer):
        return lax.rem(peer // 2, 8)

    def to_planes(low, high, chunk):
        def send(i):
            peer = seq_peer(i)

            @pl.when((z_of(peer) >= low) & (z_of(peer) < high))
            def _():
                send_back(peer, *chunk)

        return send

    back_rows(0, 16)
    each_peer(lambda i: send_back(seq_peer(i), *BACK[0]), SEQ, 5)
    lax.fori_loop(1, 3, back_more, 0)
    back_rows(80, 48)
    for low, high, n in LAST:
        each_peer(to_planes(low, high, BACK[n]), SEQ, 5)

    for i in (3, 7):
        loads[i].wait()

    def gate_tiles(i, c):
        first = i * TILES
        vals = short_conv(0, first)
        for k in range(TILES):
            gate[:, pl.ds(pl.multiple_of((first + k) * 128, 128), 128)] = vals[k].astype(BF16)
        return c

    lax.fori_loop(0, 128 // TILES, gate_tiles, 0)
    def sums_of(start, rows, sem):
        part = sqa.at[pl.ds(0, CHAN - 1), pl.ds(pl.multiple_of(start, 16), rows)]
        return pltpu.make_async_copy(part, part, sem)

    def combine(n, start, rows):
        all_of(rb, start, rows, y_recv.at[n]).wait()
        span = pl.ds(pl.multiple_of(start, 16), rows)

        def spread_row(ch, c):
            flat[pl.ds(start * 32 + ch, rows, stride=32), :] = rb[ch, span, :].astype(F32)
            return c

        lax.fori_loop(0, 32, spread_row, 0, unroll=8)

        def tile(r, c):
            p = start + r
            cols = pl.ds(pl.multiple_of(p * 128, 128), 128)
            long_out = flat[pl.ds(pl.multiple_of(p * 32, 32), 32), :]
            hidden = (res[:, cols].astype(F32) + gate[:, cols].astype(F32) * long_out).astype(BF16)
            hb[:, cols] = hidden
            wide = hidden.astype(F32)
            sqp[pl.ds(p, 1), :] = jnp.sum(wide * wide, axis=0, keepdims=True)
            return c

        lax.fori_loop(0, rows, tile, 0, unroll=8)

        def send(i):
            pltpu.make_async_remote_copy(
                src_ref=sqp.at[span],
                dst_ref=sqa.at[mc, span],
                send_sem=s_send.at[n],
                recv_sem=s_recv.at[n],
                device_id={"chan": chan_peer(i)},
                device_id_type=MESH,
            ).start()

        each_peer(send, CHAN, 7)
        sqa[mc, span, :] = sqp[span, :]

    def norm(n, start, rows):
        sums_of(start, rows, s_recv.at[n]).wait()
        span = pl.ds(pl.multiple_of(start, 16), rows)
        total = sqa[0, span, :]
        for k in range(1, CHAN):
            total = total + sqa[k, span, :]
        rs[span, :] = lax.rsqrt(total * (1.0 / (32 * CHAN)) + 1e-06)

        def tile(r, c):
            p = start + r
            cols = pl.ds(pl.multiple_of(p * 128, 128), 128)
            nb[:, cols] = (hb[:, cols].astype(F32) * (wb[9] * rs[pl.ds(p, 1), :])).astype(BF16)
            return c

        lax.fori_loop(0, rows, tile, 0, unroll=8)

    def combine_more(n, c):
        combine(n, n * 32 - 16, 32)
        return c

    def norm_more(n, c):
        norm(n, n * 32 - 16, 32)
        return c

    combine(0, 0, 16)
    lax.fori_loop(1, 4, combine_more, 0)
    combine(4, 112, 16)
    norm(0, 0, 16)
    lax.fori_loop(1, 4, norm_more, 0)
    norm(4, 112, 16)
    for n, start, rows in THERE:
        all_of(xb, start, rows, x_send.at[n]).wait()
    for n, start, rows in BACK:
        all_of(rb, start, rows, y_send.at[n]).wait()
        sums_of(start, rows, s_send.at[n]).wait()


PARTS = 4


def finish(hb, nb, out_h, out_n, out_sem):
    copies = []
    for j in range(PARTS):
        cols = pl.ds(j * (SLAB // PARTS), SLAB // PARTS)
        copies.append(pltpu.make_async_copy(hb.at[:, cols], out_h.at[:, cols], out_sem.at[0, j]))
        copies.append(pltpu.make_async_copy(nb.at[:, cols], out_n.at[:, cols], out_sem.at[1, j]))
    for copy in copies:
        copy.start()
    for copy in copies:
        copy.wait()


def per_device(streams, conv_weights, skip, filter_spec, residual, gain):
    tables = [jnp.asarray(t) for t in make_tables()]
    h2 = filter_spec.reshape(2, 8192, 128).transpose(1, 0, 2).reshape(16384, 128)
    far = pl.BlockSpec(memory_space=pl.ANY)
    near = pl.BlockSpec(memory_space=pltpu.VMEM)
    slab = (32, SLAB)
    dma = pltpu.SemaphoreType.DMA
    vmem = pltpu.VMEM
    hidden, normed = pl.pallas_call(
        fused,
        out_shape=[vmem(slab, BF16)] * 2,
        in_specs=[far, near, pl.BlockSpec(memory_space=pltpu.SMEM), far, far, near] + [far] * 5,
        out_specs=[near, near],
        scratch_shapes=[
            vmem((3, 32, 128 + SLAB), BF16),
            vmem((4096, 128), F32),
            vmem((32, 128, 128), BF16),
            vmem((32, 128, 128), BF16),
            vmem((16384, 128), BF16),
            vmem((SLOTS * 256, 128), F32),
            vmem((ROWS, 2, 128, 128), F32),
            vmem((ROWS, 256, 128), BF16),
            vmem((ROWS, 256, 128), F32),
            vmem((2, 256, 256), BF16),
            vmem((2, 128, 128), F32),
            vmem((ROWS, 2, 128, 128), F32),
            vmem((4 * SLOTS, 128), BF16),
            vmem((512, 256), BF16),
            vmem((32, 128, 128), BF16),
            vmem((32, 128, 128), BF16),
            vmem(slab, BF16),
            vmem(slab, BF16),
            vmem((128, 128), F32),
            vmem((CHAN, 128, 128), F32),
            vmem((128, 128), F32),
            vmem((10, 32, 128), F32),
            dma((5,)),
            dma((8,)),
            dma((2,)),
            dma((5,)),
            dma((5,)),
            dma((5,)),
            dma((5,)),
            dma((5,)),
            dma((5,)),
        ],
        compiler_params=pltpu.CompilerParams(
            collective_id=0, has_side_effects=True, vmem_limit_bytes=60 * 2**20
        ),
        cost_estimate=pl.CostEstimate(
            flops=8 * 10**9, bytes_accessed=20 * 2**20, transcendentals=0
        ),
    )(streams, conv_weights.transpose(0, 2, 1), skip, h2, residual, gain.reshape(1, 32), *tables)
    return pl.pallas_call(
        finish,
        out_shape=[jax.ShapeDtypeStruct(slab, BF16)] * 2,
        in_specs=[near, near],
        out_specs=[far, far],
        scratch_shapes=[
            dma((2, PARTS)),
        ],
        compiler_params=pltpu.CompilerParams(vmem_limit_bytes=32 * 2**20),
        cost_estimate=pl.CostEstimate(
            flops=0, bytes_accessed=4 * 2**20, transcendentals=0
        ),
    )(hidden, normed)


def solution(mesh):
    in_specs = (
        P(None, "chan", "seq"),
        P(None, "chan", None),
        P("chan"),
        P("chan", "seq", None, None),
        P("chan", "seq"),
        P("chan"),
    )
    return jax.shard_map(
        lambda *args: tuple(per_device(*args)),
        mesh=mesh,
        in_specs=in_specs,
        out_specs=(P("chan", "seq"), P("chan", "seq")),
        check_vma=False,
    )
```

```python
import math
import numpy as np
import jax
import jax.numpy as jnp
from jax import lax
from jax.experimental import pallas as pl
from jax.experimental.pallas import tpu as pltpu
import ml_dtypes
from jax.sharding import PartitionSpec as P

F32 = jnp.float32
BF16 = jnp.bfloat16
ROWS = 33
SLOTS = 40


def make_tables():
    d = np.arange(128)
    ang = -2.0 * np.pi * ((d[:, None] * d[None, :]) % 128) / 128
    fr, fi = np.cos(ang), np.sin(ang)
    u = np.block([[fr, -fi], [fi, fr]])
    tables = np.stack([u, u.T]).astype(ml_dtypes.bfloat16)
    ang = -2.0 * np.pi * (d[:, None] * d[None, :]) / 16384
    t0 = np.stack([np.cos(ang), np.sin(ang)]).astype(np.float32)
    place = np.arange(16384).reshape(128, 128)
    ang = -2.0 * np.pi * (np.arange(ROWS)[:, None, None] * place[None]) / 1048576
    w1 = np.stack([np.cos(ang), np.sin(ang)], axis=1).astype(np.float32)
    pick = np.zeros((2, 2, SLOTS, 128))
    perm = np.zeros((2, 2, 64, 2, 2, 128))
    for lo in range(2):
        for k1 in range(ROWS):
            alone = k1 in (0, 32)
            pick[0, lo, k1, lo * 64 + k1] = 2.0 ** -20 if alone else 2.0 ** -21
            if not alone:
                pick[1, lo, k1, lo * 64 + 64 - k1] = 2.0 ** -21
        for hi in range(64):
            k2 = 2 * hi + lo
            for part in range(2):
                perm[0, lo, hi, part, part, k2] = 1.0
                perm[1, lo, hi, part, part, 127 - k2] = 1.0 - 2.0 * part
    pick = pick.reshape(4 * SLOTS, 128).astype(ml_dtypes.bfloat16)
    perm = perm.reshape(512, 256).astype(ml_dtypes.bfloat16)
    return tables, t0, w1, pick, perm


def times(a, b, conj=False):
    if conj:
        return (a[0] * b[0] + a[1] * b[1], a[1] * b[0] - a[0] * b[1])
    return (a[0] * b[0] - a[1] * b[1], a[0] * b[1] + a[1] * b[0])


def turn(z, k, n, orient):
    re, im = z
    if k == 0:
        return z
    if 4 * k == n:
        if im is None:
            return (None, re if orient > 0 else -re)
        return (-im, re) if orient > 0 else (im, -re)
    c = math.cos(2.0 * math.pi * k / n)
    s = orient * math.sin(2.0 * math.pi * k / n)
    if im is None:
        return (re * c, re * s)
    if 8 * k == n:
        if orient > 0:
            return ((re - im) * c, (re + im) * c)
        return ((re + im) * c, (im - re) * c)
    return (re * c - im * s, re * s + im * c)


def plus(a, b):
    if a is None:
        return b
    if b is None:
        return a
    return a + b


def minus(a, b):
    if b is None:
        return a
    if a is None:
        return -b
    return a - b


def real_forward(vals, n):
    if n == 2:
        return [(vals[0], None), (vals[0], None)]
    even = real_forward(vals[0::2], n // 2)
    odd = real_forward(vals[1::2], n // 2)
    out = [None] * (n // 2 + 1)
    for k in range(n // 4 + 1):
        t = turn(odd[k], k, n, -1)
        e = even[k]
        out[k] = (plus(e[0], t[0]), plus(e[1], t[1]))
        if n // 2 - k != k:
            out[n // 2 - k] = (minus(e[0], t[0]), minus(t[1], e[1]))
    return out


def real_inverse(bins, n):
    if n == 2:
        return [bins[0][0] + bins[1][0]]
    even, odd = [], []
    for k in range(n // 4 + 1):
        a, b = bins[k], bins[n // 2 - k]
        even.append((plus(a[0], b[0]), minus(a[1], b[1])))
        t = (minus(a[0], b[0]), plus(a[1], b[1]))
        if k == n // 4:
            even[-1] = (a[0] + a[0], None)
            t = (None, a[1] + a[1])
            odd.append(turn_imag(t[1]))
        else:
            odd.append(turn(t, k, n, 1))
    first = real_inverse(even, n // 2)
    second = real_inverse(odd, n // 2)
    out = [None] * (n // 2)
    out[0::2] = first
    out[1::2] = second
    return out


def turn_imag(im):
    return (-im, None)


def filter_step(pairs_at, h_at, sh, pick, perm, direct):
    pieces = []
    for a, b in pairs_at:
        got = {}
        for name, k3 in (("a", a), ("b", b)):
            got[name] = lax.dot_general(
                pick, h_at(k3), (((1,), (1,)), ((), ())), preferred_element_type=F32
            ).astype(BF16)
        for mine, other in (("a", "b"), ("b", "a")):
            own, mirror = got[mine], got[other]
            pieces.append(
                jnp.concatenate(
                    [
                        own[0:SLOTS],
                        own[SLOTS : 2 * SLOTS],
                        mirror[2 * SLOTS : 3 * SLOTS],
                        mirror[3 * SLOTS : 4 * SLOTS],
                    ],
                    axis=1,
                )
            )
    joined = jnp.concatenate(pieces, axis=0)
    z = jnp.dot(joined, perm, preferred_element_type=F32)
    i = 0
    for a, b in pairs_at:
        for k3 in (a, b):
            zz = z[i * SLOTS : (i + 1) * SLOTS]
            sh[pl.ds(k3, SLOTS, stride=256), :] = zz[:, :128] + direct
            sh[pl.ds(128 + k3, SLOTS, stride=256), :] = zz[:, 128:]
            i += 1


def filter_prep(h_ref, sh, hs, pick_ref, perm_ref, direct, unroll=8):
    pick = pick_ref[...]
    perm = perm_ref[...]

    def h_at(k3):
        return h_ref[pl.ds(pl.multiple_of(k3 * 128, 128), 128), :]

    def step(i, c):
        filter_step(
            [(i * unroll + j, 127 - (i * unroll + j)) for j in range(unroll)],
            h_at, sh, pick, perm, direct,
        )
        return c

    lax.fori_loop(0, 64 // unroll, step, 0)

    same = (
        lax.broadcasted_iota(jnp.int32, (128, 128), 0)
        == lax.broadcasted_iota(jnp.int32, (128, 128), 1)
    ).astype(BF16)

    def turn_over(i, c):
        planes = []
        for j in range(11):
            row = pl.multiple_of((i * 11 + j) * 256, 256)
            planes.append(sh[pl.ds(row, 256), :].astype(BF16))
        turned = [
            lax.dot_general(same, x, (((1,), (1,)), ((), ())), preferred_element_type=F32)
            for x in planes
        ]
        for j in range(11):
            for part in range(2):
                hs[i * 11 + j, part] = turned[j][:, part * 128 : (part + 1) * 128]
        return c

    lax.fori_loop(0, ROWS // 11, turn_over, 0)


def stage_one(load, a_ref, w1_ref, row, height=16):
    bins = real_forward([load(s) for s in range(32)], 64)
    for k1 in range(ROWS):
        re, im = bins[k1]
        if k1 == 0:
            im = jnp.zeros_like(re)
        else:
            wr = w1_ref[k1, 0, pl.ds(row, height), :]
            wi = w1_ref[k1, 1, pl.ds(row, height), :]
            if im is None:
                re, im = re * wr, re * wi
            else:
                re, im = times((re, im), (wr, wi))
        a_ref[k1, pl.ds(row, height), :] = re.astype(BF16)
        a_ref[k1, pl.ds(128 + row, height), :] = im.astype(BF16)


def middle(groups, a_ref, g_ref, hs, u, v, t0_ref):
    tr, ti = t0_ref[0], t0_ref[1]

    def along_lanes(re, im):
        return jnp.concatenate([re.astype(BF16), im.astype(BF16)], axis=1)

    b = [
        jnp.dot(
            u, jnp.concatenate([a_ref[k] for k in rows], axis=1), preferred_element_type=F32
        )
        for rows in groups
    ]
    lines = []
    for rows, x in zip(groups, b):
        lines.append(
            jnp.concatenate(
                [
                    along_lanes(
                        *times(
                            (x[:128, i * 128 : (i + 1) * 128], x[128:, i * 128 : (i + 1) * 128]),
                            (tr, ti),
                        )
                    )
                    for i in range(len(rows))
                ],
                axis=0,
            )
        )
    c = [jnp.dot(x, v, preferred_element_type=F32) for x in lines]
    lines = []
    for rows, x in zip(groups, c):
        lines.append(
            jnp.concatenate(
                [
                    along_lanes(
                        *times(
                            (x[i * 128 : (i + 1) * 128, :128], x[i * 128 : (i + 1) * 128, 128:]),
                            (hs[k, 0], hs[k, 1]),
                        )
                    )
                    for i, k in enumerate(rows)
                ],
                axis=0,
            )
        )
    e = [jnp.dot(x, u, preferred_element_type=F32) for x in lines]
    lines = []
    for rows, x in zip(groups, e):
        cols = []
        for i in range(len(rows)):
            re, im = times(
                (x[i * 128 : (i + 1) * 128, :128], x[i * 128 : (i + 1) * 128, 128:]),
                (tr, ti),
                conj=True,
            )
            cols.append(jnp.concatenate([re.astype(BF16), im.astype(BF16)], axis=0))
        lines.append(jnp.concatenate(cols, axis=1))
    g = [jnp.dot(v, x, preferred_element_type=F32) for x in lines]
    for rows, x in zip(groups, g):
        for i, k in enumerate(rows):
            g_ref[k] = x[:, i * 128 : (i + 1) * 128]


def all_middle(a_ref, g_ref, hs, uv_ref, t0_ref):
    u, v = uv_ref[0], uv_ref[1]
    pairs = [[2 * i, 2 * i + 1] for i in range(16)]
    middle(pairs[:8], a_ref, g_ref, hs, u, v, t0_ref)
    middle(pairs[8:] + [[32]], a_ref, g_ref, hs, u, v, t0_ref)


def stage_last(g_ref, w1_ref, row, height=16):
    bins = []
    for k1 in range(ROWS):
        re = g_ref[k1, pl.ds(row, height), :]
        im = g_ref[k1, pl.ds(128 + row, height), :]
        if k1 == 0:
            bins.append((re, None))
            continue
        wr = w1_ref[k1, 0, pl.ds(row, height), :]
        wi = w1_ref[k1, 1, pl.ds(row, height), :]
        if k1 == 32:
            bins.append((re * wr + im * wi, None))
        else:
            bins.append(times((re, im), (wr, wi), conj=True))
    return real_inverse(bins, 64)


SEQ = 32
CHAN = 8
SLAB = 16384
TILES = 8
MESH = pl.DeviceIdType.MESH
THERE = [(0, 112, 16), (1, 80, 32), (2, 48, 32), (3, 16, 32), (4, 0, 16)]
BACK = [(0, 0, 16), (1, 16, 32), (2, 48, 32), (3, 80, 32), (4, 112, 16)]
LAST = [(0, 1, 3), (0, 1, 4), (1, 3, 3), (1, 3, 4), (3, 8, 3), (3, 8, 4)]


def each_peer(fn, count, per):
    def step(i, c):
        for k in range(per):
            fn(i * per + k + 1)
        return c

    whole = (count - 1) // per
    lax.fori_loop(0, whole, step, 0)
    for i in range(whole * per + 1, count):
        fn(i)


def fused(
    streams, wts, skip, h2, residual, gain, uv_in, t0_in, w1_in, pick_in, perm_in,
    hb, nb,
    st, flat, sb, xb, hv, sh, hs, a, g, uv, t0, w1, pick, perm, yb, rb,
    gate, res, sqp, sqa, rs, wb,
    piece_sem, load_sem, halo_sem, x_send, x_recv, y_send, y_recv, s_send, s_recv,
):
    me = lax.axis_index("seq")
    mc = lax.axis_index("chan")

    def seq_peer(i):
        return lax.rem(me + i * 11, SEQ)

    def chan_peer(i):
        return lax.rem(mc + i, CHAN)

    def stream_piece(n, first, tiles):
        here = pl.ds(first * 128, tiles * 128)
        there = pl.ds(first * 128 + 128, tiles * 128)
        return pltpu.make_async_copy(
            streams.at[pl.ds(1, 2), :, here], st.at[pl.ds(1, 2), :, there], piece_sem.at[n]
        )

    pieces = [
        stream_piece(0, 111, 17),
        stream_piece(1, 79, 32),
        stream_piece(2, 47, 32),
        stream_piece(3, 15, 32),
        stream_piece(4, 0, 15),
    ]
    loads = [
        pltpu.make_async_copy(h2, hv, load_sem.at[0]),
        pltpu.make_async_copy(pick_in, pick, load_sem.at[1]),
        pltpu.make_async_copy(perm_in, perm, load_sem.at[2]),
        pltpu.make_async_copy(
            streams.at[pl.ds(0, 1)], st.at[pl.ds(0, 1), :, pl.ds(128, SLAB)], load_sem.at[3]
        ),
        pltpu.make_async_copy(w1_in, w1, load_sem.at[4]),
        pltpu.make_async_copy(uv_in, uv, load_sem.at[5]),
        pltpu.make_async_copy(t0_in, t0, load_sem.at[6]),
        pltpu.make_async_copy(residual, res, load_sem.at[7]),
    ]
    pieces[0].start()

    barrier = pltpu.get_barrier_semaphore()

    def greet_seq(i):
        pl.semaphore_signal(
            barrier, inc=1, device_id={"seq": lax.rem(me + i, SEQ)}, device_id_type=MESH
        )

    def greet_chan(i):
        pl.semaphore_signal(barrier, inc=1, device_id={"chan": chan_peer(i)}, device_id_type=MESH)

    each_peer(greet_seq, SEQ, 5)
    each_peer(greet_chan, CHAN, 7)
    for copy in pieces[1:]:
        copy.start()

    eye = lax.broadcasted_iota(jnp.int32, (32, 32), 0) == lax.broadcasted_iota(
        jnp.int32, (32, 32), 1
    )

    def spread(row):
        column = jnp.sum(jnp.where(eye, row, 0.0), axis=1, keepdims=True)
        return jnp.broadcast_to(column, (32, 128))

    for stream in range(3):
        for tap in range(3):
            wb[stream * 3 + tap] = spread(wts[stream, pl.ds(tap, 1), :])
    wb[9] = spread(gain[...])

    lane = lax.broadcasted_iota(jnp.int32, (32, 128), 1)

    def short_conv(stream, first):
        cur = [
            st[stream, :, pl.ds(pl.multiple_of((first + i) * 128, 128), 128)].astype(F32)
            for i in range(TILES + 1)
        ]
        one = [pltpu.roll(t, 1, 1) for t in cur]
        two = [pltpu.roll(t, 2, 1) for t in cur]
        out = []
        for i in range(1, TILES + 1):
            back1 = jnp.where(lane < 1, one[i - 1], one[i])
            back2 = jnp.where(lane < 2, two[i - 1], two[i])
            out.append(
                wb[stream * 3] * cur[i] + wb[stream * 3 + 1] * back1 + wb[stream * 3 + 2] * back2
            )
        return out

    def gate_rows(start, rows):
        def gate_in(i, c):
            first = start + i * TILES
            one, two = short_conv(1, first), short_conv(2, first)
            for k in range(TILES):
                flat[pl.ds(pl.multiple_of((first + k) * 32, 32), 32), :] = one[k] * two[k]
            return c

        lax.fori_loop(0, rows // TILES, gate_in, 0)

    def one_row(start, rows, c):
        return flat[pl.ds(start * 32 + c, rows, stride=32), :].astype(BF16)

    def prepare(start, rows):
        span = pl.ds(pl.multiple_of(start, 16), rows)

        def take(c):
            sb[c, span, :] = one_row(start, rows, c)

        def step(i, c):
            for k in range(4):
                take(i * 4 + k)
            return c

        lax.fori_loop(0, 8, step, 0)
        xb[me, span, :] = sb[me, span, :]

    def send_to(peer, n, start, rows):
        span = pl.ds(pl.multiple_of(start, 16), rows)
        pltpu.make_async_remote_copy(
            src_ref=sb.at[peer, span],
            dst_ref=xb.at[me, span],
            send_sem=x_send.at[n],
            recv_sem=x_recv.at[n],
            device_id={"seq": peer},
            device_id_type=MESH,
        ).start()

    def send_rows(core, n, start, rows):
        def send(i):
            send_to(lax.rem(me // 2 + i * 5, SEQ // 2) * 2 + core, n, start, rows)

        each_peer(send, SEQ // 2, 5)

    def first_sends(n, start, rows):
        send_rows(0, n, start, rows)
        send_to(me + 1 - 2 * lax.rem(me, 2), n, start, rows)

    pieces[0].wait()
    gate_rows(112, 16)
    prepare(112, 16)
    pl.semaphore_wait(barrier, SEQ + CHAN - 2)
    first_sends(0, 112, 16)
    halo = pltpu.make_async_remote_copy(
        src_ref=streams.at[:, :, pl.ds(SLAB - 128, 128)],
        dst_ref=st.at[:, :, pl.ds(0, 128)],
        send_sem=halo_sem.at[0],
        recv_sem=halo_sem.at[1],
        device_id={"seq": lax.rem(me + 1, SEQ)},
        device_id_type=MESH,
    )
    halo.start()
    for i in range(1, 5):
        pieces[i].wait()
    for copy in loads:
        copy.start()

    def send_more(n, c):
        start = 112 - n * 32
        gate_rows(start, 32)
        prepare(start, 32)
        first_sends(n, start, 32)
        return c

    lax.fori_loop(1, 4, send_more, 0)
    halo.wait()
    rim = st[:, :, pl.ds(0, 128)]
    st[:, :, pl.ds(0, 128)] = jnp.where(me > 0, rim, jnp.zeros_like(rim))
    gate_rows(0, 16)
    prepare(0, 16)
    first_sends(4, 0, 16)

    def second_sends(n, c):
        send_rows(1, n, 112 - n * 32, 32)
        return c

    send_rows(1, 0, 112, 16)
    lax.fori_loop(1, 4, second_sends, 0)
    send_rows(1, 4, 0, 16)

    for i in (0, 1, 2):
        loads[i].wait()
    filter_prep(hv, sh, hs, pick, perm, skip[me] * 2.0**-20)
    for i in (4, 5, 6):
        loads[i].wait()

    def all_of(buf, start, rows, sem):
        part = buf.at[pl.ds(0, SEQ - 1), pl.ds(pl.multiple_of(start, 16), rows)]
        return pltpu.make_async_copy(part, part, sem)

    def transform_rows(n, start, rows):
        all_of(xb, start, rows, x_recv.at[n]).wait()

        def part(k, c):
            r = pl.multiple_of(start + k * 16, 16)
            stage_one(lambda s: xb[s, pl.ds(r, 16), :].astype(F32), a, w1, r)
            return c

        lax.fori_loop(0, rows // 16, part, 0)

    def transform_more(n, c):
        transform_rows(n, 112 - n * 32, 32)
        return c

    transform_rows(0, 112, 16)
    lax.fori_loop(1, 4, transform_more, 0)
    transform_rows(4, 0, 16)
    all_middle(a, g, hs, uv, t0)

    def back_rows(start, rows):
        def part(k, c):
            r = pl.multiple_of(start + k * 16, 16)
            ys = stage_last(g, w1, r)
            for s in range(SEQ):
                yb[s, pl.ds(r, 16), :] = ys[s].astype(BF16)
            return c

        lax.fori_loop(0, rows // 16, part, 0)
        span = pl.ds(pl.multiple_of(start, 16), rows)
        rb[me, span, :] = yb[me, span, :]

    def send_back(peer, n, start, rows):
        span = pl.ds(pl.multiple_of(start, 16), rows)
        pltpu.make_async_remote_copy(
            src_ref=yb.at[peer, span],
            dst_ref=rb.at[me, span],
            send_sem=y_send.at[n],
            recv_sem=y_recv.at[n],
            device_id={"seq": peer},
            device_id_type=MESH,
        ).start()

    def back_more(n, c):
        start = n * 32 - 16
        back_rows(start, 32)
        each_peer(lambda i: send_back(seq_peer(i), n, start, 32), SEQ, 5)
        return c

    def z_of(peer):
        return lax.rem(peer // 2, 8)

    def to_planes(low, high, chunk):
        def send(i):
            peer = seq_peer(i)

            @pl.when((z_of(peer) >= low) & (z_of(peer) < high))
            def _():
                send_back(peer, *chunk)

        return send

    back_rows(0, 16)
    each_peer(lambda i: send_back(seq_peer(i), *BACK[0]), SEQ, 5)
    lax.fori_loop(1, 3, back_more, 0)
    back_rows(80, 48)
    for low, high, n in LAST:
        each_peer(to_planes(low, high, BACK[n]), SEQ, 5)

    for i in (3, 7):
        loads[i].wait()

    def gate_tiles(i, c):
        first = i * TILES
        vals = short_conv(0, first)
        for k in range(TILES):
            gate[:, pl.ds(pl.multiple_of((first + k) * 128, 128), 128)] = vals[k].astype(BF16)
        return c

    lax.fori_loop(0, 128 // TILES, gate_tiles, 0)
    def sums_of(start, rows, sem):
        part = sqa.at[pl.ds(0, CHAN - 1), pl.ds(pl.multiple_of(start, 16), rows)]
        return pltpu.make_async_copy(part, part, sem)

    def combine(n, start, rows):
        all_of(rb, start, rows, y_recv.at[n]).wait()
        span = pl.ds(pl.multiple_of(start, 16), rows)

        def spread_row(ch, c):
            flat[pl.ds(start * 32 + ch, rows, stride=32), :] = rb[ch, span, :].astype(F32)
            return c

        lax.fori_loop(0, 32, spread_row, 0, unroll=8)

        def tile(r, c):
            p = start + r
            cols = pl.ds(pl.multiple_of(p * 128, 128), 128)
            long_out = flat[pl.ds(pl.multiple_of(p * 32, 32), 32), :]
            hidden = (res[:, cols].astype(F32) + gate[:, cols].astype(F32) * long_out).astype(BF16)
            hb[:, cols] = hidden
            wide = hidden.astype(F32)
            sqp[pl.ds(p, 1), :] = jnp.sum(wide * wide, axis=0, keepdims=True)
            return c

        lax.fori_loop(0, rows, tile, 0, unroll=8)

        def send(i):
            pltpu.make_async_remote_copy(
                src_ref=sqp.at[span],
                dst_ref=sqa.at[mc, span],
                send_sem=s_send.at[n],
                recv_sem=s_recv.at[n],
                device_id={"chan": chan_peer(i)},
                device_id_type=MESH,
            ).start()

        each_peer(send, CHAN, 7)
        sqa[mc, span, :] = sqp[span, :]

    def norm(n, start, rows):
        sums_of(start, rows, s_recv.at[n]).wait()
        span = pl.ds(pl.multiple_of(start, 16), rows)
        total = sqa[0, span, :]
        for k in range(1, CHAN):
            total = total + sqa[k, span, :]
        rs[span, :] = lax.rsqrt(total * (1.0 / (32 * CHAN)) + 1e-06)

        def tile(r, c):
            p = start + r
            cols = pl.ds(pl.multiple_of(p * 128, 128), 128)
            nb[:, cols] = (hb[:, cols].astype(F32) * (wb[9] * rs[pl.ds(p, 1), :])).astype(BF16)
            return c

        lax.fori_loop(0, rows, tile, 0, unroll=8)

    def combine_more(n, c):
        combine(n, n * 32 - 16, 32)
        return c

    def norm_more(n, c):
        norm(n, n * 32 - 16, 32)
        return c

    combine(0, 0, 16)
    lax.fori_loop(1, 4, combine_more, 0)
    combine(4, 112, 16)
    norm(0, 0, 16)
    lax.fori_loop(1, 4, norm_more, 0)
    norm(4, 112, 16)
    for n, start, rows in THERE:
        all_of(xb, start, rows, x_send.at[n]).wait()
    for n, start, rows in BACK:
        all_of(rb, start, rows, y_send.at[n]).wait()
        sums_of(start, rows, s_send.at[n]).wait()


PARTS = 4


def finish(hb, nb, out_h, out_n, out_sem):
    copies = []
    for j in range(PARTS):
        cols = pl.ds(j * (SLAB // PARTS), SLAB // PARTS)
        copies.append(pltpu.make_async_copy(hb.at[:, cols], out_h.at[:, cols], out_sem.at[0, j]))
        copies.append(pltpu.make_async_copy(nb.at[:, cols], out_n.at[:, cols], out_sem.at[1, j]))
    for copy in copies:
        copy.start()
    for copy in copies:
        copy.wait()


def per_device(streams, conv_weights, skip, filter_spec, residual, gain):
    tables = [jnp.asarray(t) for t in make_tables()]
    h2 = filter_spec.reshape(2, 8192, 128).transpose(1, 0, 2).reshape(16384, 128)
    far = pl.BlockSpec(memory_space=pl.ANY)
    near = pl.BlockSpec(memory_space=pltpu.VMEM)
    slab = (32, SLAB)
    dma = pltpu.SemaphoreType.DMA
    vmem = pltpu.VMEM
    hidden, normed = pl.pallas_call(
        fused,
        out_shape=[vmem(slab, BF16)] * 2,
        in_specs=[far, near, pl.BlockSpec(memory_space=pltpu.SMEM), far, far, near] + [far] * 5,
        out_specs=[near, near],
        scratch_shapes=[
            vmem((3, 32, 128 + SLAB), BF16),
            vmem((4096, 128), F32),
            vmem((32, 128, 128), BF16),
            vmem((32, 128, 128), BF16),
            vmem((16384, 128), BF16),
            vmem((SLOTS * 256, 128), F32),
            vmem((ROWS, 2, 128, 128), F32),
            vmem((ROWS, 256, 128), BF16),
            vmem((ROWS, 256, 128), F32),
            vmem((2, 256, 256), BF16),
            vmem((2, 128, 128), F32),
            vmem((ROWS, 2, 128, 128), F32),
            vmem((4 * SLOTS, 128), BF16),
            vmem((512, 256), BF16),
            vmem((32, 128, 128), BF16),
            vmem((32, 128, 128), BF16),
            vmem(slab, BF16),
            vmem(slab, BF16),
            vmem((128, 128), F32),
            vmem((CHAN, 128, 128), F32),
            vmem((128, 128), F32),
            vmem((10, 32, 128), F32),
            dma((5,)),
            dma((8,)),
            dma((2,)),
            dma((5,)),
            dma((5,)),
            dma((5,)),
            dma((5,)),
            dma((5,)),
            dma((5,)),
        ],
        compiler_params=pltpu.CompilerParams(
            collective_id=0, has_side_effects=True, vmem_limit_bytes=60 * 2**20
        ),
        cost_estimate=pl.CostEstimate(
            flops=8 * 10**9, bytes_accessed=20 * 2**20, transcendentals=0
        ),
    )(streams, conv_weights.transpose(0, 2, 1), skip, h2, residual, gain.reshape(1, 32), *tables)
    return pl.pallas_call(
        finish,
        out_shape=[jax.ShapeDtypeStruct(slab, BF16)] * 2,
        in_specs=[near, near],
        out_specs=[far, far],
        scratch_shapes=[
            dma((2, PARTS)),
        ],
        compiler_params=pltpu.CompilerParams(vmem_limit_bytes=32 * 2**20),
        cost_estimate=pl.CostEstimate(
            flops=0, bytes_accessed=4 * 2**20, transcendentals=0
        ),
    )(hidden, normed)


def solution(mesh):
    in_specs = (
        P(None, "chan", "seq"),
        P(None, "chan", None),
        P("chan"),
        P("chan", "seq", None, None),
        P("chan", "seq"),
        P("chan"),
    )
    return jax.shard_map(
        lambda *args: tuple(per_device(*args)),
        mesh=mesh,
        in_specs=in_specs,
        out_specs=(P("chan", "seq"), P("chan", "seq")),
        check_vma=False,
    )
```
